256 devices in a mesh: dp: 16 (over z, core), head: 16 (over x, y).
Axes of the slice: x: 4, y: 4, z: 8, core: 2. Of those that a mesh axis runs over, the one named last changes fastest.
Arguments:
- layer_input: bfloat16 [32768, 8192], P(('dp', 'head')), may hold values from -6 to 6
- queries: bfloat16 [32768, 4096], P(('dp', 'head')), may hold values from -8 to 8
- key_rows: bfloat16 [32768, 512], P(('dp', 'head')), may hold values from -8 to 8
- value_rows: bfloat16 [32768, 512], P(('dp', 'head')), may hold values from -6 to 6
- d_out: bfloat16 [32768, 4096], P(('dp', 'head')), may hold values from -6 to 6
- doc_lengths: int32 [16, 8], P('dp'), may hold values from 1 to 1024, 2048 in all within a row
Outputs:
- grad_q: bfloat16 [32768, 4096], P(('dp', 'head'))
- grad_wk: float32 [8192, 512], P(('dp', 'head'))
- grad_wv: float32 [8192, 512], P(('dp', 'head'))
The draws below stay inside these ranges and needn't reach their ends.
Inputs may be any that keep to these rules, and one draw needn't show every extreme that they name: `doc_lengths`: each row sums to 2048; its longest document has exactly 1024 positions.
All inputs are finite; a program needn't handle non-finite values.
Results may differ from the reference program's by a relative error of at most 0.025.
Values may be sent and summed in bfloat16 or wider, within the bound.
No kernel may reach another device: no remote copies, remote signals or barrier semaphores. Data moves between devices by JAX's collectives and lax.ppermute only.
A program may use at most 128 MiB of HBM per device.

```python
import math
import jax
import jax.numpy as jnp
import numpy as np
from jax import lax

D = 8192
HQ = 32
HK = 4
HD = 128
NDOC = 8
TOK_DEV = 128
L = 2048
WINDOWS = 16
TOKENS = 32768


def draw_queries(key, part):
    key = jax.random.fold_in(key, 11)
    group = HQ // HK
    values = jnp.clip(jax.random.normal(key, (TOKENS, HK, group, HD)), -6.0, 6.0)
    return values.reshape(TOKENS, HQ * HD).astype(jnp.bfloat16)


def draw_key_rows(key, part):
    key = jax.random.fold_in(key, 23)
    values = jnp.clip(jax.random.normal(key, (TOKENS, HK, HD)), -6.0, 6.0)
    return values.reshape(TOKENS, HK * HD).astype(jnp.bfloat16)


def levels(own_key, dims, shards, low, top_value):
    level, own = 1.0, jax.random.fold_in(own_key, 6)
    for axis_at, shards_of in shards:
        draws = jnp.exp(jax.random.uniform(jax.random.fold_in(own, axis_at), (shards_of,), jnp.float32, low / len(shards), top_value / len(shards)))
        level = level * jnp.repeat(draws, dims[axis_at] // shards_of).reshape([-1 if axis == axis_at else 1 for axis in range(len(dims))])
    return level


def profile(count, total, limit, skew):
    weights = [(1 << 20) // math.isqrt(grade ** skew) + 1 for grade in range(2, count + 1)]
    surplus, given = total - limit - (count - 1), [1] * (count - 1)
    while surplus > 0:
        movable = [i for i in range(count - 1) if given[i] < limit]
        pool, remaining = sum([weights[i] for i in movable]), surplus
        for i in movable:
            extra = min(limit - given[i], max(1, remaining * weights[i] // pool), surplus)
            given[i] = given[i] + extra
            surplus = surplus - extra
    return np.array([limit] + given)


def uneven(stream_key, number_of, total, most, slope):
    if number_of == 2:
        one = jax.random.randint(stream_key, (), max(1, total - most), min(most, total - 1) + 1)
        return jnp.stack([one, total - one])
    lengths = jnp.asarray(profile(number_of, total, most, slope), jnp.int32)
    couples = (number_of - 1) // 2
    source_of, receiver = lengths[1:1 + 2 * couples:2], lengths[2:2 + 2 * couples:2]
    slack = jnp.minimum(source_of - 1, most - receiver)
    passed = jax.random.randint(jax.random.fold_in(stream_key, 1), (couples,), 0, 1 << 20) % (slack + 1)
    lengths = lengths.at[1:1 + 2 * couples:2].set(source_of - passed).at[2:2 + 2 * couples:2].set(receiver + passed)
    return lengths[jax.random.permutation(jax.random.fold_in(stream_key, 2), number_of)]


def noise(stream_key, shape, deviation, most, cuts=(), kind=jnp.bfloat16):
    factor_of = levels(stream_key, shape, cuts, -0.22, 0.18) if cuts else 1.0
    result = jax.random.normal(stream_key, shape, jnp.float32) * deviation * factor_of
    return jnp.minimum(jnp.maximum(result, -most), most).astype(kind)


def setup_inputs(seed: int = 0) -> dict:
    streams_of = jax.random.split(jax.random.key(seed), 7)
    layer_input = noise(streams_of[0], (TOKENS, D), 1.0, 6.0, ((0, 256),))
    queries = draw_queries(jax.random.fold_in(streams_of[6], 71), 0)
    key_rows = draw_key_rows(jax.random.fold_in(streams_of[6], 71), 0)
    value_rows = noise(streams_of[3], (TOKENS, HK * HD), 1.0, 6.0, ((0, 256),))
    d_out = noise(streams_of[4], (TOKENS, HQ * HD), 1.0, 6.0, ((0, 256),))
    doc_lengths = jax.vmap(lambda own: uneven(own, NDOC, L, L // 2, 2))(jax.random.split(streams_of[5], WINDOWS)).reshape((WINDOWS, NDOC)).astype(jnp.int32)
    return dict(layer_input=layer_input, queries=queries, key_rows=key_rows, value_rows=value_rows, d_out=d_out, doc_lengths=doc_lengths)


def allowed_pairs(window_lengths):
    doc_ends = jnp.cumsum(window_lengths)
    positions = jnp.arange(L, dtype=jnp.int32)
    doc_id = jnp.sum((positions[:, None] >= doc_ends[None, :]).astype(jnp.int32), axis=1)
    same = (doc_id[:, None] == doc_id[None, :]) & (positions[:, None] >= positions[None, :])
    return same.astype(jnp.int32)


def group_grads(pieces, allowed):
    q_grp, k_one, v_one, do_grp = pieces
    scale = HD ** -0.5
    q_f = q_grp.astype(jnp.float32)
    k_f = k_one.astype(jnp.float32)
    v_f = v_one.astype(jnp.float32)
    do_f = do_grp.astype(jnp.float32)
    scores = jnp.einsum("qgd,kd->gqk", q_f, k_f) * scale
    scores = jnp.where(allowed[None] == 1, scores, -jnp.inf)
    row_max = jnp.max(scores, axis=-1, keepdims=True)
    shifted = jnp.exp(scores - row_max)
    probs = shifted / jnp.sum(shifted, axis=-1, keepdims=True)
    probs_b = lax.optimization_barrier(probs.astype(jnp.bfloat16))
    dprob = jnp.einsum("qgd,kd->gqk", do_f, v_f)
    row_dot = jnp.sum(probs * dprob, axis=-1, keepdims=True)
    dscore = lax.optimization_barrier((probs * (dprob - row_dot)).astype(jnp.bfloat16))
    ds_f = dscore.astype(jnp.float32)
    grad_q = (jnp.einsum("gqk,kd->qgd", ds_f, k_f) * scale).astype(jnp.bfloat16)
    grad_k = jnp.einsum("gqk,qgd->kd", ds_f, q_f) * scale
    grad_v = jnp.einsum("gqk,qgd->kd", probs_b.astype(jnp.float32), do_f)
    return grad_q, grad_k, grad_v


def window_grads(pieces):
    q_w, k_w, v_w, do_w, window_lengths = pieces
    allowed = allowed_pairs(window_lengths)
    group = HQ // HK
    q_four = q_w.reshape(L, HK, group, HD).transpose(1, 0, 2, 3)
    do_four = do_w.reshape(L, HK, group, HD).transpose(1, 0, 2, 3)
    k_three = k_w.reshape(L, HK, HD).transpose(1, 0, 2)
    v_three = v_w.reshape(L, HK, HD).transpose(1, 0, 2)
    grad_q, grad_k, grad_v = lax.map(lambda item: group_grads(item, allowed), (q_four, k_three, v_three, do_four))
    grad_q = grad_q.transpose(1, 0, 2, 3).reshape(L, HQ * HD)
    grad_k = grad_k.astype(jnp.bfloat16).transpose(1, 0, 2).reshape(L, HK * HD)
    grad_v = grad_v.astype(jnp.bfloat16).transpose(1, 0, 2).reshape(L, HK * HD)
    return grad_q, grad_k, grad_v


def reference(layer_input, queries, key_rows, value_rows, d_out, doc_lengths):
    grad_q, dk_b, dv_b = lax.map(window_grads, (queries.reshape(WINDOWS, L, HQ * HD), key_rows.reshape(WINDOWS, L, HK * HD), value_rows.reshape(WINDOWS, L, HK * HD), d_out.reshape(WINDOWS, L, HQ * HD), doc_lengths))
    grad_q = grad_q.reshape(TOKENS, HQ * HD)
    blocks = TOKENS // TOK_DEV
    x_rows = layer_input.reshape(blocks, TOK_DEV, D)
    dk_rows = dk_b.reshape(blocks, TOK_DEV, HK * HD)
    dv_rows = dv_b.reshape(blocks, TOK_DEV, HK * HD)

    def add_block(totals, pieces):
        x_part, k_part, v_part = pieces
        term_k = jnp.dot(x_part.T, k_part, preferred_element_type=jnp.float32)
        term_v = jnp.dot(x_part.T, v_part, preferred_element_type=jnp.float32)
        term_k = lax.optimization_barrier(term_k.astype(jnp.bfloat16)).astype(jnp.float32)
        term_v = lax.optimization_barrier(term_v.astype(jnp.bfloat16)).astype(jnp.float32)
        return (totals[0] + term_k, totals[1] + term_v), None

    empty = jnp.zeros((D, HK * HD), jnp.float32)
    (grad_wk, grad_wv), unused = lax.scan(add_block, (empty, empty), (x_rows, dk_rows, dv_rows))
    return grad_q, grad_wk, grad_wv
```

```python
import functools
import math

import jax
import jax.numpy as jnp
from jax import lax
from jax.experimental import pallas as pl
from jax.experimental.pallas import tpu as pltpu
from jax.sharding import PartitionSpec as P

HQ = 32
HK = 4
HD = 128
BLK = 128
KB = 256
NX = 4
NY = 4
NZ = 8
NC = 2
MAX_KB = 5
SCALE = HD ** (-0.5)
LOG2E = math.log2(math.e)
BF = jnp.bfloat16
F32 = jnp.float32
AXES = ("dp", "head")
VM = pl.BlockSpec(memory_space=pltpu.VMEM)
SM = pl.BlockSpec(memory_space=pltpu.SMEM)


def send(value, dx=0, dy=0, dc=0):
    pairs = []
    for z in range(NZ):
        for c in range(NC):
            for x in range(NX):
                for y in range(NY):
                    src = ((z * NC + c) * NX + x) * NY + y
                    dst = ((z * NC + (c + dc) % NC) * NX + (x + dx) % NX) * NY + (y + dy) % NY
                    pairs.append((src, dst))
    return lax.ppermute(value, AXES, pairs)


def call(kernel, outs, ins, scratch=(), flops=0, moved=0, limit=56, smem=1):
    return pl.pallas_call(
        kernel,
        out_shape=outs,
        in_specs=[SM] * smem + [VM] * (len(ins) - smem),
        out_specs=[VM] * len(outs),
        scratch_shapes=list(scratch),
        compiler_params=pltpu.CompilerParams(vmem_limit_bytes=limit * 1024 * 1024),
        cost_estimate=pl.CostEstimate(flops=flops, bytes_accessed=moved, transcendentals=0),
    )(*ins)


def sds(shape, dtype=BF):
    return jax.ShapeDtypeStruct(shape, dtype)


def pack_kv_kernel(at, k, v, *outs):
    for s in range(NX):
        first = pl.multiple_of(lax.rem(at[0] + s, NX) * HD, HD)
        outs[s][:, 0:HD] = k[:, pl.ds(first, HD)]
        outs[s][:, HD : 2 * HD] = v[:, pl.ds(first, HD)]


def pack_heads_kernel(at, q, do, *outs):
    group = HQ // HK
    for s in range(NX):
        first = lax.rem(at[0] + s, NX) * (group * HD)
        for h in range(group):
            col = pl.multiple_of(first + h * HD, HD)
            outs[s][0, h * BLK : (h + 1) * BLK, :] = q[:, pl.ds(col, HD)]
            outs[s][1, h * BLK : (h + 1) * BLK, :] = do[:, pl.ds(col, HD)]


def pack_x_kernel(at, li, *outs):
    for s in range(NX):
        for d in range(NC):
            core = lax.rem(at[2] + d, NC)
            for z in range(NZ):
                col = z * (NC * 512) + core * 512 + lax.rem(at[0] + s, NX) * BLK
                outs[2 * s + d][:, z * BLK : (z + 1) * BLK] = li[:, pl.ds(pl.multiple_of(col, BLK), BLK)]


def turn_x_kernel(at, *refs):
    out = refs[-1]
    for d in range(NC):
        for s in range(NX):
            spot = pl.multiple_of(d * 512 + lax.rem(at[0] - s + NX, NX) * BLK, BLK)
            for z in range(NZ):
                rows = pl.ds(z * BLK, BLK)
                out[rows, pl.ds(spot, BLK)] = refs[2 * s + d][:, z * BLK : (z + 1) * BLK].T


def attention_kernel(at, lens, *refs):
    qd_in, kv_in = refs[0:4], refs[4:8]
    dq_out, r_out = refs[8:12], refs[12:16]
    qd, k_all, v_all, kt_all, s_all, dp_all, pb, dsb, dqt, dk, dv, dq_all = refs[16:]
    x, y = at[0], at[1]
    group = HQ // HK
    rows_n = group * BLK
    chunks = [slice(i * KB, (i + 1) * KB) for i in range(rows_n // KB)]
    nt = (((1,), (1,)), ((), ()))

    for s in range(NY):
        for t in range(NX):
            blk = NY * lax.rem(x - t + NX, NX) + lax.rem(y - s + NY, NY)
            rows = pl.ds(pl.multiple_of(blk * BLK, BLK), BLK)
            k_piece = kv_in[s][t * BLK : (t + 1) * BLK, 0:HD]
            k_all[rows, :] = k_piece
            v_all[rows, :] = kv_in[s][t * BLK : (t + 1) * BLK, HD : 2 * HD]
            kt_all[lax.div(blk, 2), :, pl.ds(pl.multiple_of(lax.rem(blk, 2) * BLK, BLK), BLK)] = k_piece.T
    for s in range(NX):
        qd[s] = qd_in[s][...]
    dk[...] = jnp.zeros_like(dk)
    dv[...] = jnp.zeros_like(dv)

    def fold(value, op):
        return op(value.reshape(KB // 8, 8, KB), axis=0)

    def query_block(j, carry):
        base = (NY * lax.rem(x - j + NX, NX) + y) * BLK
        q_pos = base + (lax.broadcasted_iota(jnp.int32, (1, KB), 1) & (BLK - 1))
        start = jnp.zeros((1, KB), jnp.int32)
        first, run = jnp.int32(0), jnp.int32(0)
        for n in range(8):
            run = run + lens[n]
            start = jnp.maximum(start, jnp.where(q_pos >= run, run, 0))
            first = jnp.maximum(first, jnp.where(base >= run, run, 0))
        lo, hi = lax.div(first, KB), lax.div(base, KB) + 1

        def scores(kb, tops):
            keys = k_all[pl.ds(pl.multiple_of(kb * KB, KB), KB), :]
            k_pos = kb * KB + lax.broadcasted_iota(jnp.int32, (KB, KB), 0)
            keep = (k_pos >= start) & (k_pos <= q_pos)
            out = []
            for i, part in enumerate(chunks):
                s = lax.dot_general(keys, qd[j, 0, part, :], nt, preferred_element_type=F32)
                s = jnp.where(keep, s, -jnp.inf)
                s_all[kb - lo, :, part] = s
                out.append(jnp.maximum(tops[i], fold(s, jnp.max)))
            return tuple(out)

        tops = lax.fori_loop(lo, hi, scores, tuple(jnp.full((8, KB), -jnp.inf, F32) for _ in chunks))
        factor = SCALE * LOG2E
        tops = [jnp.max(t, axis=0, keepdims=True) * factor for t in tops]

        def weights(kb, sums):
            vals = v_all[pl.ds(pl.multiple_of(kb * KB, KB), KB), :]
            total, dots = [], []
            for i, part in enumerate(chunks):
                dp = lax.dot_general(vals, qd[j, 1, part, :], nt, preferred_element_type=F32)
                p = jnp.exp2(s_all[kb - lo, :, part] * factor - tops[i])
                s_all[kb - lo, :, part] = p
                dp_all[kb - lo, :, part] = dp
                total.append(sums[0][i] + fold(p, jnp.sum))
                dots.append(sums[1][i] + fold(p * dp, jnp.sum))
            return tuple(total), tuple(dots)

        zero = tuple(jnp.zeros((8, KB), F32) for _ in chunks)
        total, dots = lax.fori_loop(lo, hi, weights, (zero, zero))
        inv = [1.0 / jnp.sum(t, axis=0, keepdims=True) for t in total]
        row_dot = [jnp.sum(d, axis=0, keepdims=True) * i for d, i in zip(dots, inv)]
        dqt[...] = jnp.zeros_like(dqt)

        def grads(kb, carry):
            rows = pl.ds(pl.multiple_of(kb * KB, KB), KB)
            for i, part in enumerate(chunks):
                p = s_all[kb - lo, :, part] * inv[i]
                pb[:, part] = p.astype(BF)
                dsb[:, part] = (p * (dp_all[kb - lo, :, part] - row_dot[i])).astype(BF)
            dv[rows, :] += jnp.dot(pb[...], qd[j, 1], preferred_element_type=F32)
            dk[rows, :] += jnp.dot(dsb[...], qd[j, 0], preferred_element_type=F32)
            dqt[...] += jnp.dot(kt_all[kb], dsb[...], preferred_element_type=F32)
            return carry

        lax.fori_loop(lo, hi, grads, 0)
        for h in range(group):
            head = slice(h * BLK, (h + 1) * BLK)
            dq_all[j, head, :] = (dqt[:, head].T * SCALE).astype(BF)
        return carry

    lax.fori_loop(0, NX, query_block, 0)
    for s in range(NX):
        dq_out[s][...] = dq_all[s]
    for s in range(NY):
        for t in range(NX):
            blk = NY * t + lax.rem(y + s, NY)
            rows = pl.ds(pl.multiple_of(blk * BLK, BLK), BLK)
            r_out[s][t * BLK : (t + 1) * BLK, 0:HD] = (dk[rows, :] * SCALE).astype(BF)
            r_out[s][t * BLK : (t + 1) * BLK, HD : 2 * HD] = dv[rows, :].astype(BF)


def join_q_kernel(at, *refs):
    out = refs[-1]
    group = HQ // HK
    for s in range(NX):
        first = lax.rem(at[0] + s, NX) * (group * HD)
        for h in range(group):
            out[:, pl.ds(pl.multiple_of(first + h * HD, HD), HD)] = refs[s][h * BLK : (h + 1) * BLK, :]


def project_kernel(pairs_n, at, xt, *refs):
    own, other = refs[0:pairs_n], refs[pairs_n : 2 * pairs_n]
    outs, acc = refs[2 * pairs_n : 2 * pairs_n + NY], refs[-1]
    for t in range(pairs_n):
        acc[...] = jnp.dot(xt[:, 0:512], own[t][...], preferred_element_type=F32) + jnp.dot(
            xt[:, 512:1024], other[t][...], preferred_element_type=F32
        )
        for s in range(NY):
            for z in range(NZ):
                row = pl.multiple_of(z * BLK + lax.rem(at[1] + s, NY) * 32, 32)
                outs[s][z, :, t * 256 : (t + 1) * 256] = acc[pl.ds(row, 32), :].astype(BF)


def finish_kernel(at, *refs):
    parts, wk, wv = refs[:-2], refs[-2], refs[-1]
    for t in range(NX):
        part = parts[t // 2]
        col = pl.multiple_of(lax.rem(at[0] - t + NX, NX) * HD, HD)
        first = (t % 2) * 256
        wk[:, pl.ds(col, HD)] = jnp.sum(part[:, :, first : first + HD].astype(F32), axis=0)
        wv[:, pl.ds(col, HD)] = jnp.sum(part[:, :, first + HD : first + 2 * HD].astype(F32), axis=0)


def total(values):
    acc = values[0].astype(F32)
    for value in values[1:]:
        acc = acc + value.astype(F32)
    return acc.astype(BF)


def on_device(layer_input, queries, key_rows, value_rows, d_out, doc_lengths):
    head, dp = lax.axis_index("head"), lax.axis_index("dp")
    at = jnp.stack([head // NY, head % NY, dp % NC, dp // NC]).astype(jnp.int32)
    with jax.named_scope("pack_kv"):
        kv = call(pack_kv_kernel, [sds((BLK, 256))] * 4, (at, key_rows, value_rows), moved=1 << 19)
    with jax.named_scope("pack_q_do"):
        qd = call(pack_heads_kernel, [sds((2, 1024, HD))] * 4, (at, queries, d_out), moved=1 << 22)
    with jax.named_scope("pack_x"):
        xp = call(pack_x_kernel, [sds((BLK, 1024))] * 8, (at, layer_input), moved=1 << 22)
    with jax.named_scope("kv_over_x"):
        kv = [kv[0]] + [send(kv[s], dx=s) for s in range(1, NX)]
        kv = jnp.concatenate(kv, axis=0)
    with jax.named_scope("q_do_over_x"):
        qd = [qd[0]] + [send(qd[s], dx=s) for s in range(1, NX)]
    with jax.named_scope("kv_over_y"):
        kv = [kv] + [send(kv, dy=s) for s in range(1, NY)]
    with jax.named_scope("x_over_x"):
        xp = [xp[i] if i == 0 else send(xp[i], dx=i // 2, dc=i % 2) for i in range(8)]
        (xt,) = call(turn_x_kernel, [sds((1024, 1024))], (at, *xp), moved=1 << 22)
    with jax.named_scope("attention"):
        outs = call(
            attention_kernel,
            [sds((1024, HD))] * 4 + [sds((512, 256))] * 4,
            (at, doc_lengths[0], *qd, *kv),
            scratch=[
                pltpu.VMEM((4, 2, 1024, HD), BF),
                pltpu.VMEM((2048, HD), BF),
                pltpu.VMEM((2048, HD), BF),
                pltpu.VMEM((8, HD, KB), BF),
                pltpu.VMEM((MAX_KB, KB, 1024), F32),
                pltpu.VMEM((MAX_KB, KB, 1024), F32),
                pltpu.VMEM((KB, 1024), BF),
                pltpu.VMEM((KB, 1024), BF),
                pltpu.VMEM((HD, 1024), F32),
                pltpu.VMEM((2048, HD), F32),
                pltpu.VMEM((2048, HD), F32),
                pltpu.VMEM((4, 1024, HD), BF),
            ],
            flops=15 * 10**9,
            moved=6 << 20,
            smem=2,
        )
    dq, terms = outs[:4], outs[4:]
    with jax.named_scope("terms_over_y"):
        dkv = total([terms[0]] + [send(terms[s], dy=s) for s in range(1, NY)])
    with jax.named_scope("dkv_over_x"):
        own = [dkv] + [send(dkv, dx=s) for s in range(1, NX)]
        other = [send(piece, dc=1) for piece in own]
    with jax.named_scope("project"):
        halves = []
        for half in range(2):
            pick = slice(2 * half, 2 * half + 2)
            partial = call(
                functools.partial(project_kernel, 2),
                [sds((NZ, 32, 512))] * 4,
                (at, xt, *own[pick], *other[pick]),
                scratch=[pltpu.VMEM((1024, 256), F32)],
                flops=10**9,
                moved=1 << 22,
            )
            with jax.named_scope("partial_over_y"):
                summed = total([partial[0]] + [send(partial[s], dy=s) for s in range(1, NY)])
            with jax.named_scope("partial_over_z"):
                groups = [[z * NC + c for z in range(NZ)] for c in range(NC)]
                halves.append(lax.all_to_all(summed, "dp", 0, 0, axis_index_groups=groups, tiled=True))
    with jax.named_scope("grad_q"):
        dq = [dq[0]] + [send(dq[s], dx=-s) for s in range(1, NX)]
        (grad_q,) = call(join_q_kernel, [sds((BLK, HQ * HD))], (at, *dq), moved=1 << 21)
    with jax.named_scope("finish"):
        wk, wv = call(finish_kernel, [sds((32, 512), F32)] * 2, (at, *halves), moved=1 << 20)
    return grad_q, wk, wv


def solution(mesh):
    spec = P(("dp", "head"), None)
    return jax.shard_map(
        on_device,
        mesh=mesh,
        in_specs=(spec, spec, spec, spec, spec, P("dp", None)),
        out_specs=(spec, spec, spec),
        check_vma=False,
    )
```

```python
import functools
import math

import jax
import jax.numpy as jnp
from jax import lax
from jax.experimental import pallas as pl
from jax.experimental.pallas import tpu as pltpu
from jax.sharding import PartitionSpec as P

HQ = 32
HK = 4
HD = 128
BLK = 128
KB = 256
NX = 4
NY = 4
NZ = 8
NC = 2
MAX_KB = 5
SCALE = HD ** (-0.5)
LOG2E = math.log2(math.e)
BF = jnp.bfloat16
F32 = jnp.float32
AXES = ("dp", "head")
VM = pl.BlockSpec(memory_space=pltpu.VMEM)
SM = pl.BlockSpec(memory_space=pltpu.SMEM)


def send(value, dx=0, dy=0, dc=0):
    pairs = []
    for z in range(NZ):
        for c in range(NC):
            for x in range(NX):
                for y in range(NY):
                    src = ((z * NC + c) * NX + x) * NY + y
                    dst = ((z * NC + (c + dc) % NC) * NX + (x + dx) % NX) * NY + (y + dy) % NY
                    pairs.append((src, dst))
    return lax.ppermute(value, AXES, pairs)


def call(kernel, outs, ins, scratch=(), flops=0, moved=0, limit=16, smem=1, late=()):
    body = kernel
    if late:
        n, skip = len(ins), len(late)
        body = lambda *refs: kernel(*refs[:n], *refs[n + skip :])
    return pl.pallas_call(
        body,
        out_shape=outs,
        in_specs=[SM] * smem + [VM] * (len(ins) - smem) + [VM] * len(late),
        out_specs=[VM] * len(outs),
        scratch_shapes=list(scratch),
        compiler_params=pltpu.CompilerParams(vmem_limit_bytes=limit * 1024 * 1024),
        cost_estimate=pl.CostEstimate(flops=flops, bytes_accessed=moved, transcendentals=0),
    )(*ins, *late)


def sds(shape, dtype=BF):
    return jax.ShapeDtypeStruct(shape, dtype)


def pack_kv_kernel(at, k, v, *outs):
    for s in range(NX):
        first = pl.multiple_of(lax.rem(at[0] + s, NX) * HD, HD)
        outs[s][:, 0:HD] = k[:, pl.ds(first, HD)]
        outs[s][:, HD : 2 * HD] = v[:, pl.ds(first, HD)]


def join_kv_kernel(at, *refs):
    for s in range(NX):
        refs[-1][s * BLK : (s + 1) * BLK, :] = refs[s][...]


def pack_heads_kernel(at, q, do, *outs):
    group = HQ // HK
    for s in range(NX):
        first = lax.rem(at[0] + s, NX) * (group * HD)
        for h in range(group):
            col = pl.multiple_of(first + h * HD, HD)
            outs[s][0, h * BLK : (h + 1) * BLK, :] = q[:, pl.ds(col, HD)]
            outs[s][1, h * BLK : (h + 1) * BLK, :] = do[:, pl.ds(col, HD)]


def pack_x_kernel(at, li, *outs):
    for s in range(NX):
        for d in range(NC):
            core = lax.rem(at[2] + d, NC)
            for z in range(NZ):
                col = z * (NC * 512) + core * 512 + lax.rem(at[0] + s, NX) * BLK
                outs[s][d, :, z * BLK : (z + 1) * BLK] = li[:, pl.ds(pl.multiple_of(col, BLK), BLK)]


def turn_x_kernel(at, *refs):
    outs = refs[NX:]
    for d in range(NC):
        for s in range(NX):
            spot = pl.multiple_of(lax.rem(at[0] - s + NX, NX) * BLK, BLK)
            for z in range(NZ):
                rows = pl.ds(z * BLK, BLK)
                outs[d][rows, pl.ds(spot, BLK)] = refs[s][d, :, z * BLK : (z + 1) * BLK].T


def attention_kernel(first_piece, at, lens, *refs):
    x, y = at[0], at[1]
    group = HQ // HK
    rows_n = group * BLK
    chunks = [slice(i * KB, (i + 1) * KB) for i in range(rows_n // KB)]
    nt = (((1,), (1,)), ((), ()))
    qd_in, refs = refs[0:2], refs[2:]
    if first_piece == 0:
        kv_in, dq_out = refs[0:4], refs[4:6]
        dk, dv, k_all, v_all, kt_all, qd, s_all, dp_all, pb, dsb, dqt, dq_all = refs[6:]
        for s in range(NY):
            for t in range(NX):
                blk = NY * lax.rem(x - t + NX, NX) + lax.rem(y - s + NY, NY)
                rows = pl.ds(pl.multiple_of(blk * BLK, BLK), BLK)
                k_piece = kv_in[s][t * BLK : (t + 1) * BLK, 0:HD]
                k_all[rows, :] = k_piece
                v_all[rows, :] = kv_in[s][t * BLK : (t + 1) * BLK, HD : 2 * HD]
                kt_all[lax.div(blk, 2), :, pl.ds(pl.multiple_of(lax.rem(blk, 2) * BLK, BLK), BLK)] = k_piece.T
        dk[...] = jnp.zeros_like(dk)
        dv[...] = jnp.zeros_like(dv)
    else:
        dk_in, dv_in, k_all, v_all, kt_all = refs[0:5]
        dq_out, r_out = refs[5:7], refs[7:11]
        qd, s_all, dp_all, pb, dsb, dqt, dq_all, dk, dv = refs[11:]
        dk[...] = dk_in[...]
        dv[...] = dv_in[...]
    for s in range(2):
        qd[s] = qd_in[s][...]

    def fold(value, op):
        return op(value.reshape(KB // 8, 8, KB), axis=0)

    def query_block(j, carry):
        base = (NY * lax.rem(x - j - first_piece + NX, NX) + y) * BLK
        q_pos = base + (lax.broadcasted_iota(jnp.int32, (1, KB), 1) & (BLK - 1))
        start = jnp.zeros((1, KB), jnp.int32)
        first, run = jnp.int32(0), jnp.int32(0)
        for n in range(8):
            run = run + lens[n]
            start = jnp.maximum(start, jnp.where(q_pos >= run, run, 0))
            first = jnp.maximum(first, jnp.where(base >= run, run, 0))
        lo, hi = lax.div(first, KB), lax.div(base, KB) + 1

        def scores(kb, tops):
            keys = k_all[pl.ds(pl.multiple_of(kb * KB, KB), KB), :]
            k_pos = kb * KB + lax.broadcasted_iota(jnp.int32, (KB, KB), 0)
            keep = (k_pos >= start) & (k_pos <= q_pos)
            out = []
            for i, part in enumerate(chunks):
                s = lax.dot_general(keys, qd[j, 0, part, :], nt, preferred_element_type=F32)
                s = jnp.where(keep, s, -jnp.inf)
                s_all[kb - lo, :, part] = s
                out.append(jnp.maximum(tops[i], fold(s, jnp.max)))
            return tuple(out)

        tops = lax.fori_loop(lo, hi, scores, tuple(jnp.full((8, KB), -jnp.inf, F32) for _ in chunks))
        factor = SCALE * LOG2E
        tops = [jnp.max(t, axis=0, keepdims=True) * factor for t in tops]

        def weights(kb, sums):
            vals = v_all[pl.ds(pl.multiple_of(kb * KB, KB), KB), :]
            total, dots = [], []
            for i, part in enumerate(chunks):
                dp = lax.dot_general(vals, qd[j, 1, part, :], nt, preferred_element_type=F32)
                p = jnp.exp2(s_all[kb - lo, :, part] * factor - tops[i])
                s_all[kb - lo, :, part] = p
                dp_all[kb - lo, :, part] = dp
                total.append(sums[0][i] + fold(p, jnp.sum))
                dots.append(sums[1][i] + fold(p * dp, jnp.sum))
            return tuple(total), tuple(dots)

        zero = tuple(jnp.zeros((8, KB), F32) for _ in chunks)
        total, dots = lax.fori_loop(lo, hi, weights, (zero, zero))
        inv = [1.0 / jnp.sum(t, axis=0, keepdims=True) for t in total]
        row_dot = [jnp.sum(d, axis=0, keepdims=True) * i for d, i in zip(dots, inv)]
        dqt[...] = jnp.zeros_like(dqt)

        def grads(kb, carry):
            rows = pl.ds(pl.multiple_of(kb * KB, KB), KB)
            for i, part in enumerate(chunks):
                p = s_all[kb - lo, :, part] * inv[i]
                pb[:, part] = p.astype(BF)
                dsb[:, part] = (p * (dp_all[kb - lo, :, part] - row_dot[i])).astype(BF)
            dv[rows, :] += jnp.dot(pb[...], qd[j, 1], preferred_element_type=F32)
            dk[rows, :] += jnp.dot(dsb[...], qd[j, 0], preferred_element_type=F32)
            dqt[...] += jnp.dot(kt_all[kb], dsb[...], preferred_element_type=F32)
            return carry

        lax.fori_loop(lo, hi, grads, 0)
        for h in range(group):
            head = slice(h * BLK, (h + 1) * BLK)
            dq_all[j, head, :] = (dqt[:, head].T * SCALE).astype(BF)
        return carry

    lax.fori_loop(0, 2, query_block, 0)
    for s in range(2):
        dq_out[s][...] = dq_all[s]
    if first_piece == 0:
        return
    for s in range(NY):
        for t in range(NX):
            blk = NY * t + lax.rem(y + s, NY)
            rows = pl.ds(pl.multiple_of(blk * BLK, BLK), BLK)
            r_out[s][t * BLK : (t + 1) * BLK, 0:HD] = (dk[rows, :] * SCALE).astype(BF)
            r_out[s][t * BLK : (t + 1) * BLK, HD : 2 * HD] = dv[rows, :].astype(BF)


def join_q_kernel(at, *refs):
    out = refs[-1]
    group = HQ // HK
    for s in range(NX):
        first = lax.rem(at[0] + s, NX) * (group * HD)
        for h in range(group):
            out[:, pl.ds(pl.multiple_of(first + h * HD, HD), HD)] = refs[s][h * BLK : (h + 1) * BLK, :]


def project_kernel(pairs_n, at, xt, xt_other, *refs):
    own, other = refs[0:pairs_n], refs[pairs_n : 2 * pairs_n]
    outs, acc = refs[2 * pairs_n : 2 * pairs_n + NY], refs[-1]
    for t in range(pairs_n):
        acc[...] = jnp.dot(xt[...], own[t][...], preferred_element_type=F32) + jnp.dot(
            xt_other[...], other[t][...], preferred_element_type=F32
        )
        for s in range(NY):
            for z in range(NZ):
                row = pl.multiple_of(z * BLK + lax.rem(at[1] + s, NY) * 32, 32)
                outs[s][z, :, t * 256 : (t + 1) * 256] = acc[pl.ds(row, 32), :].astype(BF)


def add_kernel(*refs):
    out, first = refs[-1], 0
    for terms in [refs[i : i + NY] for i in range(0, len(refs) - 1, NY)]:
        wide = terms[0].shape[2]
        for z in range(NZ):
            acc = terms[0][z].astype(F32)
            for term in terms[1:]:
                acc = acc + term[z].astype(F32)
            out[z, :, first : first + wide] = acc.astype(BF)
        first += wide


def finish_kernel(at, part, wk, wv):
    for t in range(NX):
        col = pl.multiple_of(lax.rem(at[0] - t + NX, NX) * HD, HD)
        first = t * 256
        wk[:, pl.ds(col, HD)] = jnp.sum(part[:, :, first : first + HD].astype(F32), axis=0)
        wv[:, pl.ds(col, HD)] = jnp.sum(part[:, :, first + HD : first + 2 * HD].astype(F32), axis=0)


def pass_kernel(n, *refs):
    for i in range(n):
        refs[i - n][...] = refs[i][...]


def after(values, first):
    n = len(values)
    outs = [sds(v.shape, v.dtype) for v in values]
    return call(functools.partial(pass_kernel, n), outs, (*values, *first), moved=1024, smem=0)


def split(n, values):
    return list(values[:n]), list(values[n:])


def total(values):
    acc = values[0].astype(F32)
    for value in values[1:]:
        acc = acc + value.astype(F32)
    return acc.astype(BF)


def on_device(layer_input, queries, key_rows, value_rows, d_out, doc_lengths):
    head, dp = lax.axis_index("head"), lax.axis_index("dp")
    at = jnp.stack([head // NY, head % NY, dp % NC, dp // NC]).astype(jnp.int32)
    with jax.named_scope("pack_kv"):
        kv = call(pack_kv_kernel, [sds((BLK, 256))] * 4, (at, key_rows, value_rows), moved=1 << 19)
    with jax.named_scope("pack_q_do"):
        qd = call(pack_heads_kernel, [sds((2, 1024, HD))] * 4, (at, queries, d_out), moved=1 << 22, late=[kv[1]])
    with jax.named_scope("kv_over_x"):
        kv = [kv[0]] + [send(kv[s], dx=s) for s in range(1, NX)]
        qd = [qd[0], *after(qd[1:], kv[1:])]
        (kv,) = call(join_kv_kernel, [sds((512, 256))], (at, *kv), moved=1 << 19, late=[qd[1]])
    with jax.named_scope("pack_x"):
        xp = call(pack_x_kernel, [sds((NC, BLK, 1024))] * 4, (at, layer_input), moved=1 << 22, late=[kv])
    with jax.named_scope("q_do_over_x"):
        qd = [qd[0]] + [send(qd[s], dx=s) for s in range(1, NX)]
    with jax.named_scope("kv_over_y"):
        kv = [kv] + [send(kv, dy=s) for s in range(1, NY)]
    with jax.named_scope("attention"):
        held = [sds((2048, HD), F32)] * 2 + [sds((2048, HD))] * 2 + [sds((8, HD, KB))]
        scratch = [
            pltpu.VMEM((2, 2, 1024, HD), BF),
            pltpu.VMEM((MAX_KB, KB, 1024), F32),
            pltpu.VMEM((MAX_KB, KB, 1024), F32),
            pltpu.VMEM((KB, 1024), BF),
            pltpu.VMEM((KB, 1024), BF),
            pltpu.VMEM((HD, 1024), F32),
            pltpu.VMEM((2, 1024, HD), BF),
        ]
        dq_a, held = split(
            2,
            call(
                functools.partial(attention_kernel, 0),
                [sds((1024, HD))] * 2 + held,
                (at, doc_lengths[0], *qd[:2], *kv),
                scratch=scratch,
                flops=8 * 10**9,
                moved=6 << 20,
                limit=32,
                smem=2,
            ),
        )
        give = after(xp[1:], [dq_a[0], qd[2]])
        xp = [xp[0]] + [send(d, dx=s + 1) for s, d in enumerate(give)]
        dq_b, terms = split(
            2,
            call(
                functools.partial(attention_kernel, 2),
                [sds((1024, HD))] * 2 + [sds((512, 256))] * 4,
                (at, doc_lengths[0], *qd[2:], *held),
                scratch=scratch + [pltpu.VMEM((2048, HD), F32)] * 2,
                flops=8 * 10**9,
                moved=6 << 20,
                limit=32,
                smem=2,
                late=give[:1],
            ),
        )
    dq = dq_a + dq_b
    with jax.named_scope("terms_over_y"):
        terms = [terms[0]] + [send(d, dy=s + 1) for s, d in enumerate(after(terms[1:], [xp[1]]))]
        dkv = total(terms)
    with jax.named_scope("turn_x"):
        xt, xt_give = call(turn_x_kernel, [sds((1024, 512))] * 2, (at, *xp), moved=1 << 22, late=terms[1:])
        xt_other = send(xt_give, dc=1)
    with jax.named_scope("dkv_over_x"):
        own = [dkv] + [send(dkv, dx=s) for s in range(1, NX)]
        other = [send(piece, dc=1) for piece in own[:2]]
    with jax.named_scope("project"):
        parts = []
        for pick in (slice(0, 1), slice(1, 4)):
            n = pick.stop - pick.start
            partial = call(
                functools.partial(project_kernel, n),
                [sds((NZ, 32, 256 * n))] * 4,
                (at, xt, xt_other, *own[pick], *other[pick]),
                scratch=[pltpu.VMEM((1024, 256), F32)],
                flops=n * 5 * 10**8,
                moved=1 << 22,

            )
            with jax.named_scope("partial_over_y"):
                parts += [partial[0]] + [send(partial[s], dy=s) for s in range(1, NY)]
            if len(other) == 2:
                other += [send(piece, dc=1) for piece in after(own[2:], parts[1:])]
    with jax.named_scope("partial_over_z"):
        dq = [dq[0]] + [send(d, dx=-s - 1) for s, d in enumerate(after(dq[1:], [parts[4]]))]
        (summed,) = call(add_kernel, [sds((NZ, 32, 1024))], parts, moved=5 << 20, smem=0, late=dq[1:])
        groups = [[z * NC + c for z in range(NZ)] for c in range(NC)]
        last = lax.all_to_all(summed, "dp", 0, 0, axis_index_groups=groups, tiled=True)
    with jax.named_scope("grad_q"):
        (grad_q,) = call(join_q_kernel, [sds((BLK, HQ * HD))], (at, *dq), moved=1 << 21)
    with jax.named_scope("finish"):
        wk, wv = call(finish_kernel, [sds((32, 512), F32)] * 2, (at, last), moved=1 << 20)
    return grad_q, wk, wv


def solution(mesh):
    spec = P(("dp", "head"), None)
    return jax.shard_map(
        on_device,
        mesh=mesh,
        in_specs=(spec, spec, spec, spec, spec, P("dp", None)),
        out_specs=(spec, spec, spec),
        check_vma=False,
    )
```

```python
import functools
import math

import jax
import jax.numpy as jnp
from jax import lax
from jax.experimental import pallas as pl
from jax.experimental.pallas import tpu as pltpu
from jax.sharding import PartitionSpec as P

HQ = 32
HK = 4
HD = 128
BLK = 128
KB = 256
NX = 4
NY = 4
NZ = 8
NC = 2
MAX_KB = 5
SCALE = HD ** (-0.5)
LOG2E = math.log2(math.e)
BF = jnp.bfloat16
F32 = jnp.float32
AXES = ("dp", "head")
VM = pl.BlockSpec(memory_space=pltpu.VMEM)
SM = pl.BlockSpec(memory_space=pltpu.SMEM)


def send(value, dx=0, dy=0, dc=0):
    pairs = []
    for z in range(NZ):
        for c in range(NC):
            for x in range(NX):
                for y in range(NY):
                    src = ((z * NC + c) * NX + x) * NY + y
                    dst = ((z * NC + (c + dc) % NC) * NX + (x + dx) % NX) * NY + (y + dy) % NY
                    pairs.append((src, dst))
    return lax.ppermute(value, AXES, pairs)


def call(kernel, outs, ins, scratch=(), flops=0, moved=0, limit=16, smem=1, late=()):
    body = kernel
    if late:
        n, skip = len(ins), len(late)
        body = lambda *refs: kernel(*refs[:n], *refs[n + skip :])
    return pl.pallas_call(
        body,
        out_shape=outs,
        in_specs=[SM] * smem + [VM] * (len(ins) - smem) + [VM] * len(late),
        out_specs=[VM] * len(outs),
        scratch_shapes=list(scratch),
        compiler_params=pltpu.CompilerParams(vmem_limit_bytes=limit * 1024 * 1024),
        cost_estimate=pl.CostEstimate(flops=flops, bytes_accessed=moved, transcendentals=0),
    )(*ins, *late)


def sds(shape, dtype=BF):
    return jax.ShapeDtypeStruct(shape, dtype)


def pack_kv_kernel(at, k, v, *outs):
    for s in range(NX):
        first = pl.multiple_of(lax.rem(at[0] + s, NX) * HD, HD)
        outs[s][:, 0:HD] = k[:, pl.ds(first, HD)]
        outs[s][:, HD : 2 * HD] = v[:, pl.ds(first, HD)]


def join_kv_kernel(at, *refs):
    for s in range(NX):
        refs[-1][s * BLK : (s + 1) * BLK, :] = refs[s][...]


def pack_heads_kernel(at, q, do, *outs):
    group = HQ // HK
    for s in range(NX):
        first = lax.rem(at[0] + s, NX) * (group * HD)
        for h in range(group):
            col = pl.multiple_of(first + h * HD, HD)
            outs[s][0, h * BLK : (h + 1) * BLK, :] = q[:, pl.ds(col, HD)]
            outs[s][1, h * BLK : (h + 1) * BLK, :] = do[:, pl.ds(col, HD)]


def pack_x_kernel(at, li, *outs):
    for s in range(NX):
        for d in range(NC):
            core = lax.rem(at[2] + d, NC)
            for z in range(NZ):
                col = z * (NC * 512) + core * 512 + lax.rem(at[0] + s, NX) * BLK
                outs[s][d, :, z * BLK : (z + 1) * BLK] = li[:, pl.ds(pl.multiple_of(col, BLK), BLK)]


def turn_x_kernel(at, *refs):
    outs = refs[NX:]
    for d in range(NC):
        for s in range(NX):
            spot = pl.multiple_of(lax.rem(at[0] - s + NX, NX) * BLK, BLK)
            for z in range(NZ):
                rows = pl.ds(z * BLK, BLK)
                outs[d][rows, pl.ds(spot, BLK)] = refs[s][d, :, z * BLK : (z + 1) * BLK].T


def attention_kernel(pieces, at, lens, *refs):
    x, y = at[0], at[1]
    group = HQ // HK
    rows_n = group * BLK
    chunks = [slice(i * KB, (i + 1) * KB) for i in range(rows_n // KB)]
    nt = (((1,), (1,)), ((), ()))
    n = len(pieces)
    qd_in, refs = refs[0:n], refs[n:]
    if n == 3:
        kv_in, dq_out = refs[0:4], refs[4:7]
        dk, dv, k_all, v_all, kt_all, qd, s_all, dp_all, pb, dsb, dqt, dq_all = refs[7:]
        for s in range(NY):
            for t in range(NX):
                blk = NY * lax.rem(x - t + NX, NX) + lax.rem(y - s + NY, NY)
                rows = pl.ds(pl.multiple_of(blk * BLK, BLK), BLK)
                k_piece = kv_in[s][t * BLK : (t + 1) * BLK, 0:HD]
                k_all[rows, :] = k_piece
                v_all[rows, :] = kv_in[s][t * BLK : (t + 1) * BLK, HD : 2 * HD]
                kt_all[lax.div(blk, 2), :, pl.ds(pl.multiple_of(lax.rem(blk, 2) * BLK, BLK), BLK)] = k_piece.T
        dk[...] = jnp.zeros_like(dk)
        dv[...] = jnp.zeros_like(dv)
    else:
        dk_in, dv_in, k_all, v_all, kt_all = refs[0:5]
        dq_out, r_out = refs[5:6], refs[6:10]
        qd, s_all, dp_all, pb, dsb, dqt, dq_all, dk, dv = refs[10:]
        dk[...] = dk_in[...]
        dv[...] = dv_in[...]
    for i in range(n):
        qd[i] = qd_in[i][...]

    def fold(value, op):
        return op(value.reshape(KB // 8, 8, KB), axis=0)

    def query_block(j, carry):
        shift = j + lax.div(j, 2) if n == 3 else pieces[0]
        base = (NY * lax.rem(x - shift + NX, NX) + y) * BLK
        q_pos = base + (lax.broadcasted_iota(jnp.int32, (1, KB), 1) & (BLK - 1))
        start = jnp.zeros((1, KB), jnp.int32)
        first, run = jnp.int32(0), jnp.int32(0)
        for doc in range(8):
            run = run + lens[doc]
            start = jnp.maximum(start, jnp.where(q_pos >= run, run, 0))
            first = jnp.maximum(first, jnp.where(base >= run, run, 0))
        lo, hi = lax.div(first, KB), lax.div(base, KB) + 1

        def scores(kb, tops):
            keys = k_all[pl.ds(pl.multiple_of(kb * KB, KB), KB), :]
            k_pos = kb * KB + lax.broadcasted_iota(jnp.int32, (KB, KB), 0)
            keep = (k_pos >= start) & (k_pos <= q_pos)
            out = []
            for i, part in enumerate(chunks):
                s = lax.dot_general(keys, qd[j, 0, part, :], nt, preferred_element_type=F32)
                s = jnp.where(keep, s, -jnp.inf)
                s_all[kb - lo, :, part] = s
                out.append(jnp.maximum(tops[i], fold(s, jnp.max)))
            return tuple(out)

        tops = lax.fori_loop(lo, hi, scores, tuple(jnp.full((8, KB), -jnp.inf, F32) for _ in chunks))
        factor = SCALE * LOG2E
        tops = [jnp.max(t, axis=0, keepdims=True) * factor for t in tops]

        def weights(kb, sums):
            vals = v_all[pl.ds(pl.multiple_of(kb * KB, KB), KB), :]
            total, dots = [], []
            for i, part in enumerate(chunks):
                dp = lax.dot_general(vals, qd[j, 1, part, :], nt, preferred_element_type=F32)
                p = jnp.exp2(s_all[kb - lo, :, part] * factor - tops[i])
                s_all[kb - lo, :, part] = p
                dp_all[kb - lo, :, part] = dp
                total.append(sums[0][i] + fold(p, jnp.sum))
                dots.append(sums[1][i] + fold(p * dp, jnp.sum))
            return tuple(total), tuple(dots)

        zero = tuple(jnp.zeros((8, KB), F32) for _ in chunks)
        total, dots = lax.fori_loop(lo, hi, weights, (zero, zero))
        inv = [1.0 / jnp.sum(t, axis=0, keepdims=True) for t in total]
        row_dot = [jnp.sum(d, axis=0, keepdims=True) * i for d, i in zip(dots, inv)]
        dqt[...] = jnp.zeros_like(dqt)

        def grads(kb, carry):
            rows = pl.ds(pl.multiple_of(kb * KB, KB), KB)
            for i, part in enumerate(chunks):
                p = s_all[kb - lo, :, part] * inv[i]
                pb[:, part] = p.astype(BF)
                dsb[:, part] = (p * (dp_all[kb - lo, :, part] - row_dot[i])).astype(BF)
            dv[rows, :] += jnp.dot(pb[...], qd[j, 1], preferred_element_type=F32)
            dk[rows, :] += jnp.dot(dsb[...], qd[j, 0], preferred_element_type=F32)
            dqt[...] += jnp.dot(kt_all[kb], dsb[...], preferred_element_type=F32)
            return carry

        lax.fori_loop(lo, hi, grads, 0)
        for h in range(group):
            head = slice(h * BLK, (h + 1) * BLK)
            dq_all[j, head, :] = (dqt[:, head].T * SCALE).astype(BF)
        return carry

    lax.fori_loop(0, n, query_block, 0)
    for i in range(n):
        dq_out[i][...] = dq_all[i]
    if n == 3:
        return
    for s in range(NY):
        for t in range(NX):
            blk = NY * t + lax.rem(y + s, NY)
            rows = pl.ds(pl.multiple_of(blk * BLK, BLK), BLK)
            r_out[s][t * BLK : (t + 1) * BLK, 0:HD] = (dk[rows, :] * SCALE).astype(BF)
            r_out[s][t * BLK : (t + 1) * BLK, HD : 2 * HD] = dv[rows, :].astype(BF)


def join_q_kernel(at, *refs):
    out = refs[-1]
    group = HQ // HK
    for s in range(NX):
        first = lax.rem(at[0] + s, NX) * (group * HD)
        for h in range(group):
            out[:, pl.ds(pl.multiple_of(first + h * HD, HD), HD)] = refs[s][h * BLK : (h + 1) * BLK, :]


def project_kernel(pairs_n, at, xt, xt_other, *refs):
    own, other = refs[0:pairs_n], refs[pairs_n : 2 * pairs_n]
    outs, acc = refs[2 * pairs_n : 2 * pairs_n + NY], refs[-1]
    for t in range(pairs_n):
        acc[...] = jnp.dot(xt[...], own[t][...], preferred_element_type=F32) + jnp.dot(
            xt_other[...], other[t][...], preferred_element_type=F32
        )
        for s in range(NY):
            for z in range(NZ):
                row = pl.multiple_of(z * BLK + lax.rem(at[1] + s, NY) * 32, 32)
                outs[s][z, :, t * 256 : (t + 1) * 256] = acc[pl.ds(row, 32), :].astype(BF)


def add_kernel(*refs):
    out, first = refs[-1], 0
    for terms in [refs[i : i + NY] for i in range(0, len(refs) - 1, NY)]:
        wide = terms[0].shape[2]
        for z in range(NZ):
            acc = terms[0][z].astype(F32)
            for term in terms[1:]:
                acc = acc + term[z].astype(F32)
            out[z, :, first : first + wide] = acc.astype(BF)
        first += wide


def finish_kernel(at, part, wk, wv):
    for t in range(NX):
        col = pl.multiple_of(lax.rem(at[0] - t + NX, NX) * HD, HD)
        first = t * 256
        wk[:, pl.ds(col, HD)] = jnp.sum(part[:, :, first : first + HD].astype(F32), axis=0)
        wv[:, pl.ds(col, HD)] = jnp.sum(part[:, :, first + HD : first + 2 * HD].astype(F32), axis=0)


def pass_kernel(n, *refs):
    for i in range(n):
        refs[i - n][...] = refs[i][...]


def after(values, first):
    n = len(values)
    outs = [sds(v.shape, v.dtype) for v in values]
    return call(functools.partial(pass_kernel, n), outs, (*values, *first), moved=1024, smem=0)


def split(n, values):
    return list(values[:n]), list(values[n:])


def sum_kernel(*refs):
    acc = refs[0][...].astype(F32)
    for ref in refs[1:NY]:
        acc = acc + ref[...].astype(F32)
    refs[-1][...] = acc.astype(BF)


def on_device(layer_input, queries, key_rows, value_rows, d_out, doc_lengths):
    head, dp = lax.axis_index("head"), lax.axis_index("dp")
    at = jnp.stack([head // NY, head % NY, dp % NC, dp // NC]).astype(jnp.int32)
    with jax.named_scope("pack_kv"):
        kv = call(pack_kv_kernel, [sds((BLK, 256))] * 4, (at, key_rows, value_rows), moved=1 << 19)
    with jax.named_scope("pack_q_do"):
        qd = call(pack_heads_kernel, [sds((2, 1024, HD))] * 4, (at, queries, d_out), moved=1 << 22, late=[kv[1]])
    with jax.named_scope("kv_over_x"):
        kv = [kv[0]] + [send(kv[s], dx=s) for s in range(1, NX)]
        qd = [qd[0], *after(qd[1:], kv[1:])]
        (kv,) = call(join_kv_kernel, [sds((512, 256))], (at, *kv), moved=1 << 19, late=[qd[1]])
    with jax.named_scope("pack_x"):
        xp = call(pack_x_kernel, [sds((NC, BLK, 1024))] * 4, (at, layer_input), moved=1 << 22, late=[kv])
    with jax.named_scope("q_do_over_x"):
        qd = [qd[0]] + [send(qd[s], dx=s) for s in range(1, NX)]
    with jax.named_scope("kv_over_y"):
        kv = [kv] + [send(kv, dy=s) for s in range(1, NY)]
    with jax.named_scope("attention"):
        held = [sds((2048, HD), F32)] * 2 + [sds((2048, HD))] * 2 + [sds((8, HD, KB))]
        def scratch(n):
            return [
                pltpu.VMEM((n, 2, 1024, HD), BF),
                pltpu.VMEM((MAX_KB, KB, 1024), F32),
                pltpu.VMEM((MAX_KB, KB, 1024), F32),
                pltpu.VMEM((KB, 1024), BF),
                pltpu.VMEM((KB, 1024), BF),
                pltpu.VMEM((HD, 1024), F32),
                pltpu.VMEM((n, 1024, HD), BF),
            ]

        (dq0, dq1, dq3), held = split(
            3,
            call(
                functools.partial(attention_kernel, (0, 1, 3)),
                [sds((1024, HD))] * 3 + held,
                (at, doc_lengths[0], qd[0], qd[1], qd[3], *kv),
                scratch=scratch(3),
                flops=12 * 10**9,
                moved=6 << 20,
                limit=32,
                smem=2,
            ),
        )
        (dq2,), terms = split(
            1,
            call(
                functools.partial(attention_kernel, (2,)),
                [sds((1024, HD))] + [sds((512, 256))] * 4,
                (at, doc_lengths[0], qd[2], *held),
                scratch=scratch(1) + [pltpu.VMEM((2048, HD), F32)] * 2,
                flops=4 * 10**9,
                moved=6 << 20,
                limit=32,
                smem=2,
            ),
        )
    dq = [dq0, dq1, dq2, dq3]
    with jax.named_scope("terms_over_y"):
        give = after(xp[1:], terms[:1])
        terms = [terms[0]] + [send(terms[s], dy=s) for s in range(1, NY)]
        xp = [xp[0]] + [send(d, dx=s + 1) for s, d in enumerate(give)]
        (dkv,) = call(sum_kernel, [sds((512, 256))], terms, moved=5 << 18, smem=0, late=[xp[1]])
    with jax.named_scope("dkv_over_x"):
        own = [dkv] + [send(dkv, dx=s) for s in range(1, NX)]
        other = [send(piece, dc=1) for piece in own]
    with jax.named_scope("turn_x"):
        xt, xt_give = call(turn_x_kernel, [sds((1024, 512))] * 2, (at, *xp), moved=1 << 22, late=own[1:])
        xt_other = send(xt_give, dc=1)
    with jax.named_scope("grad_q"):
        dq = [dq[0]] + [send(d, dx=-s - 1) for s, d in enumerate(after(dq[1:], own[1:]))]
    with jax.named_scope("project"):
        parts = []
        for pick in (slice(0, 2), slice(2, 4)):
            n = pick.stop - pick.start
            partial = call(
                functools.partial(project_kernel, n),
                [sds((NZ, 32, 256 * n))] * 4,
                (at, xt, xt_other, *own[pick], *other[pick]),
                scratch=[pltpu.VMEM((1024, 256), F32)],
                flops=n * 5 * 10**8,
                moved=1 << 22,
                late=parts[:1] + dq[1:] if parts else [],
            )
            with jax.named_scope("partial_over_y"):
                parts += [partial[0]] + [send(partial[s], dy=s) for s in range(1, NY)]
    with jax.named_scope("partial_over_z"):
        (summed,) = call(add_kernel, [sds((NZ, 32, 1024))], parts, moved=5 << 20, smem=0)
        groups = [[z * NC + c for z in range(NZ)] for c in range(NC)]
        last = lax.all_to_all(summed, "dp", 0, 0, axis_index_groups=groups, tiled=True)
    with jax.named_scope("grad_q"):
        (grad_q,) = call(join_q_kernel, [sds((BLK, HQ * HD))], (at, *dq), moved=1 << 21)
    with jax.named_scope("finish"):
        wk, wv = call(finish_kernel, [sds((32, 512), F32)] * 2, (at, last), moved=1 << 20)
    return grad_q, wk, wv


def solution(mesh):
    spec = P(("dp", "head"), None)
    return jax.shard_map(
        on_device,
        mesh=mesh,
        in_specs=(spec, spec, spec, spec, spec, P("dp", None)),
        out_specs=(spec, spec, spec),
        check_vma=False,
    )
```

```python
import functools
import math

import jax
import jax.numpy as jnp
from jax import lax
from jax.experimental import pallas as pl
from jax.experimental.pallas import tpu as pltpu
from jax.sharding import PartitionSpec as P

HQ = 32
HK = 4
HD = 128
BLK = 128
KB = 256
NX = 4
NY = 4
NZ = 8
NC = 2
MAX_KB = 5
SCALE = HD ** (-0.5)
LOG2E = math.log2(math.e)
BF = jnp.bfloat16
F32 = jnp.float32
AXES = ("dp", "head")
VM = pl.BlockSpec(memory_space=pltpu.VMEM)
SM = pl.BlockSpec(memory_space=pltpu.SMEM)


def send(value, dx=0, dy=0, dc=0):
    pairs = []
    for z in range(NZ):
        for c in range(NC):
            for x in range(NX):
                for y in range(NY):
                    src = ((z * NC + c) * NX + x) * NY + y
                    dst = ((z * NC + (c + dc) % NC) * NX + (x + dx) % NX) * NY + (y + dy) % NY
                    pairs.append((src, dst))
    return lax.ppermute(value, AXES, pairs)


def call(kernel, outs, ins, scratch=(), flops=0, moved=0, limit=16, smem=1, late=()):
    body = kernel
    if late:
        n, skip = len(ins), len(late)
        body = lambda *refs: kernel(*refs[:n], *refs[n + skip :])
    return pl.pallas_call(
        body,
        out_shape=outs,
        in_specs=[SM] * smem + [VM] * (len(ins) - smem) + [VM] * len(late),
        out_specs=[VM] * len(outs),
        scratch_shapes=list(scratch),
        compiler_params=pltpu.CompilerParams(vmem_limit_bytes=limit * 1024 * 1024),
        cost_estimate=pl.CostEstimate(flops=flops, bytes_accessed=moved, transcendentals=0),
    )(*ins, *late)


def sds(shape, dtype=BF):
    return jax.ShapeDtypeStruct(shape, dtype)


def pack_kv_kernel(at, k, v, *outs):
    for s in range(NX):
        first = pl.multiple_of(lax.rem(at[0] + s, NX) * HD, HD)
        outs[s][:, 0:HD] = k[:, pl.ds(first, HD)]
        outs[s][:, HD : 2 * HD] = v[:, pl.ds(first, HD)]


def join_kv_kernel(at, *refs):
    for s in range(NX):
        refs[-1][s * BLK : (s + 1) * BLK, :] = refs[s][...]


def pack_heads_kernel(at, q, do, *outs):
    group = HQ // HK
    for s in range(NX):
        first = lax.rem(at[0] + s, NX) * (group * HD)
        for h in range(group):
            col = pl.multiple_of(first + h * HD, HD)
            outs[s][0, h * BLK : (h + 1) * BLK, :] = q[:, pl.ds(col, HD)]
            outs[s][1, h * BLK : (h + 1) * BLK, :] = do[:, pl.ds(col, HD)]


def pack_x_kernel(at, li, *outs):
    for s in range(NX):
        for d in range(NC):
            core = lax.rem(at[2] + d, NC)
            for z in range(NZ):
                col = z * (NC * 512) + core * 512 + lax.rem(at[0] + s, NX) * BLK
                outs[s][d, :, z * BLK : (z + 1) * BLK] = li[:, pl.ds(pl.multiple_of(col, BLK), BLK)]


def turn_x_kernel(at, *refs):
    outs = refs[NX:]
    for d in range(NC):
        for s in range(NX):
            spot = pl.multiple_of(lax.rem(at[0] - s + NX, NX) * BLK, BLK)
            for z in range(NZ):
                rows = pl.ds(z * BLK, BLK)
                outs[d][rows, pl.ds(spot, BLK)] = refs[s][d, :, z * BLK : (z + 1) * BLK].T


def attention_kernel(pieces, at, lens, *refs):
    x, y = at[0], at[1]
    group = HQ // HK
    rows_n = group * BLK
    chunks = [slice(i * KB, (i + 1) * KB) for i in range(rows_n // KB)]
    nt = (((1,), (1,)), ((), ()))
    n = len(pieces)
    qd_in, refs = refs[0:n], refs[n:]
    if n == 3:
        kv_in, dq_out = refs[0:4], refs[4:7]
        dk, dv, k_all, v_all, kt_all, qd, s_all, dp_all, pb, dsb, dqt, dq_all = refs[7:]
        for s in range(NY):
            for t in range(NX):
                blk = NY * lax.rem(x - t + NX, NX) + lax.rem(y - s + NY, NY)
                rows = pl.ds(pl.multiple_of(blk * BLK, BLK), BLK)
                k_piece = kv_in[s][t * BLK : (t + 1) * BLK, 0:HD]
                k_all[rows, :] = k_piece
                v_all[rows, :] = kv_in[s][t * BLK : (t + 1) * BLK, HD : 2 * HD]
                kt_all[lax.div(blk, 2), :, pl.ds(pl.multiple_of(lax.rem(blk, 2) * BLK, BLK), BLK)] = k_piece.T
        dk[...] = jnp.zeros_like(dk)
        dv[...] = jnp.zeros_like(dv)
    else:
        dk_in, dv_in, k_all, v_all, kt_all = refs[0:5]
        dq_out, r_out = refs[5:6], refs[6:10]
        qd, s_all, dp_all, pb, dsb, dqt, dq_all, dk, dv = refs[10:]
        dk[...] = dk_in[...]
        dv[...] = dv_in[...]
    for i in range(n):
        qd[i] = qd_in[i][...]

    def fold(value, op):
        return op(value.reshape(KB // 8, 8, KB), axis=0)

    def query_block(j, carry):
        shift = j + lax.div(j, 2) if n == 3 else pieces[0]
        base = (NY * lax.rem(x - shift + NX, NX) + y) * BLK
        q_pos = base + (lax.broadcasted_iota(jnp.int32, (1, KB), 1) & (BLK - 1))
        start = jnp.zeros((1, KB), jnp.int32)
        first, run = jnp.int32(0), jnp.int32(0)
        for doc in range(8):
            run = run + lens[doc]
            start = jnp.maximum(start, jnp.where(q_pos >= run, run, 0))
            first = jnp.maximum(first, jnp.where(base >= run, run, 0))
        lo, hi = lax.div(first, KB), lax.div(base, KB) + 1

        def scores(kb, tops):
            keys = k_all[pl.ds(pl.multiple_of(kb * KB, KB), KB), :]
            k_pos = kb * KB + lax.broadcasted_iota(jnp.int32, (KB, KB), 0)
            keep = (k_pos >= start) & (k_pos <= q_pos)
            out = []
            for i, part in enumerate(chunks):
                s = lax.dot_general(keys, qd[j, 0, part, :], nt, preferred_element_type=F32)
                s = jnp.where(keep, s, -jnp.inf)
                s_all[kb - lo, :, part] = s
                out.append(jnp.maximum(tops[i], fold(s, jnp.max)))
            return tuple(out)

        tops = lax.fori_loop(lo, hi, scores, tuple(jnp.full((8, KB), -jnp.inf, F32) for _ in chunks))
        factor = SCALE * LOG2E
        tops = [jnp.max(t, axis=0, keepdims=True) * factor for t in tops]

        def weights(kb, sums):
            vals = v_all[pl.ds(pl.multiple_of(kb * KB, KB), KB), :]
            total, dots = [], []
            for i, part in enumerate(chunks):
                dp = lax.dot_general(vals, qd[j, 1, part, :], nt, preferred_element_type=F32)
                p = jnp.exp2(s_all[kb - lo, :, part] * factor - tops[i])
                s_all[kb - lo, :, part] = p
                dp_all[kb - lo, :, part] = dp
                total.append(sums[0][i] + fold(p, jnp.sum))
                dots.append(sums[1][i] + fold(p * dp, jnp.sum))
            return tuple(total), tuple(dots)

        zero = tuple(jnp.zeros((8, KB), F32) for _ in chunks)
        total, dots = lax.fori_loop(lo, hi, weights, (zero, zero))
        inv = [1.0 / jnp.sum(t, axis=0, keepdims=True) for t in total]
        row_dot = [jnp.sum(d, axis=0, keepdims=True) * i for d, i in zip(dots, inv)]
        dqt[...] = jnp.zeros_like(dqt)

        def grads(kb, carry):
            rows = pl.ds(pl.multiple_of(kb * KB, KB), KB)
            for i, part in enumerate(chunks):
                p = s_all[kb - lo, :, part] * inv[i]
                pb[:, part] = p.astype(BF)
                dsb[:, part] = (p * (dp_all[kb - lo, :, part] - row_dot[i])).astype(BF)
            dv[rows, :] += jnp.dot(pb[...], qd[j, 1], preferred_element_type=F32)
            dk[rows, :] += jnp.dot(dsb[...], qd[j, 0], preferred_element_type=F32)
            dqt[...] += jnp.dot(kt_all[kb], dsb[...], preferred_element_type=F32)
            return carry

        lax.fori_loop(lo, hi, grads, 0)
        for h in range(group):
            head = slice(h * BLK, (h + 1) * BLK)
            dq_all[j, head, :] = (dqt[:, head].T * SCALE).astype(BF)
        return carry

    lax.fori_loop(0, n, query_block, 0)
    for i in range(n):
        dq_out[i][...] = dq_all[i]
    if n == 3:
        return
    for s in range(NY):
        for t in range(NX):
            blk = NY * t + lax.rem(y + s, NY)
            rows = pl.ds(pl.multiple_of(blk * BLK, BLK), BLK)
            r_out[s][t * BLK : (t + 1) * BLK, 0:HD] = (dk[rows, :] * SCALE).astype(BF)
            r_out[s][t * BLK : (t + 1) * BLK, HD : 2 * HD] = dv[rows, :].astype(BF)


def join_q_kernel(at, *refs):
    out = refs[-1]
    group = HQ // HK
    for s in range(NX):
        first = lax.rem(at[0] + s, NX) * (group * HD)
        for h in range(group):
            out[:, pl.ds(pl.multiple_of(first + h * HD, HD), HD)] = refs[s][h * BLK : (h + 1) * BLK, :]


def project_kernel(pairs_n, at, xt, xt_other, *refs):
    own, other = refs[0:pairs_n], refs[pairs_n : 2 * pairs_n]
    outs, acc = refs[2 * pairs_n : 2 * pairs_n + NY], refs[-1]
    for t in range(pairs_n):
        acc[...] = jnp.dot(xt[...], own[t][...], preferred_element_type=F32) + jnp.dot(
            xt_other[...], other[t][...], preferred_element_type=F32
        )
        for s in range(NY):
            for z in range(NZ):
                row = pl.multiple_of(z * BLK + lax.rem(at[1] + s, NY) * 32, 32)
                outs[s][z, :, t * 256 : (t + 1) * 256] = acc[pl.ds(row, 32), :].astype(BF)


def add_kernel(*refs):
    out, first = refs[-1], 0
    for terms in [refs[i : i + NY] for i in range(0, len(refs) - 1, NY)]:
        wide = terms[0].shape[2]
        for z in range(NZ):
            acc = terms[0][z].astype(F32)
            for term in terms[1:]:
                acc = acc + term[z].astype(F32)
            out[z, :, first : first + wide] = acc.astype(BF)
        first += wide


def finish_kernel(at, part, wk, wv):
    for t in range(NX):
        col = pl.multiple_of(lax.rem(at[0] - t + NX, NX) * HD, HD)
        first = t * 256
        wk[:, pl.ds(col, HD)] = jnp.sum(part[:, :, first : first + HD].astype(F32), axis=0)
        wv[:, pl.ds(col, HD)] = jnp.sum(part[:, :, first + HD : first + 2 * HD].astype(F32), axis=0)


def pass_kernel(n, *refs):
    for i in range(n):
        refs[i - n][...] = refs[i][...]


def after(values, first):
    n = len(values)
    outs = [sds(v.shape, v.dtype) for v in values]
    return call(functools.partial(pass_kernel, n), outs, (*values, *first), moved=1024, smem=0)


def split(n, values):
    return list(values[:n]), list(values[n:])


def sum_kernel(*refs):
    acc = refs[0][...].astype(F32)
    for ref in refs[1:NY]:
        acc = acc + ref[...].astype(F32)
    refs[-1][...] = acc.astype(BF)


def on_device(layer_input, queries, key_rows, value_rows, d_out, doc_lengths):
    head, dp = lax.axis_index("head"), lax.axis_index("dp")
    at = jnp.stack([head // NY, head % NY, dp % NC, dp // NC]).astype(jnp.int32)
    with jax.named_scope("pack_kv"):
        kv = call(pack_kv_kernel, [sds((BLK, 256))] * 4, (at, key_rows, value_rows), moved=1 << 19)
    with jax.named_scope("pack_q_do"):
        qd = call(pack_heads_kernel, [sds((2, 1024, HD))] * 4, (at, queries, d_out), moved=1 << 22, late=[kv[1]])
    with jax.named_scope("kv_over_x"):
        kv = [kv[0]] + [send(kv[s], dx=s) for s in range(1, NX)]
        qd = [qd[0], *after(qd[1:], kv[1:])]
        (kv,) = call(join_kv_kernel, [sds((512, 256))], (at, *kv), moved=1 << 19, late=[qd[1]])
    with jax.named_scope("pack_x"):
        xp = call(pack_x_kernel, [sds((NC, BLK, 1024))] * 4, (at, layer_input), moved=1 << 22, late=[kv])
    with jax.named_scope("q_do_over_x"):
        qd = [qd[0]] + [send(qd[s], dx=s) for s in range(1, NX)]
    with jax.named_scope("kv_over_y"):
        kv = [kv] + [send(kv, dy=s) for s in range(1, NY)]
    with jax.named_scope("attention"):
        held = [sds((2048, HD), F32)] * 2 + [sds((2048, HD))] * 2 + [sds((8, HD, KB))]
        def scratch(n):
            return [
                pltpu.VMEM((n, 2, 1024, HD), BF),
                pltpu.VMEM((MAX_KB, KB, 1024), F32),
                pltpu.VMEM((MAX_KB, KB, 1024), F32),
                pltpu.VMEM((KB, 1024), BF),
                pltpu.VMEM((KB, 1024), BF),
                pltpu.VMEM((HD, 1024), F32),
                pltpu.VMEM((n, 1024, HD), BF),
            ]

        (dq0, dq1, dq3), held = split(
            3,
            call(
                functools.partial(attention_kernel, (0, 1, 3)),
                [sds((1024, HD))] * 3 + held,
                (at, doc_lengths[0], qd[0], qd[1], qd[3], *kv),
                scratch=scratch(3),
                flops=12 * 10**9,
                moved=6 << 20,
                limit=32,
                smem=2,
            ),
        )
        (dq2,), terms = split(
            1,
            call(
                functools.partial(attention_kernel, (2,)),
                [sds((1024, HD))] + [sds((512, 256))] * 4,
                (at, doc_lengths[0], qd[2], *held),
                scratch=scratch(1) + [pltpu.VMEM((2048, HD), F32)] * 2,
                flops=4 * 10**9,
                moved=6 << 20,
                limit=32,
                smem=2,
            ),
        )
    dq = [dq0, dq1, dq2, dq3]
    with jax.named_scope("terms_over_y"):
        give = after(xp[1:], terms[:1])
        terms = [terms[0]] + [send(terms[s], dy=s) for s in range(1, NY)]
        xp = [xp[0]] + [send(d, dx=s + 1) for s, d in enumerate(give)]
        (dkv,) = call(sum_kernel, [sds((512, 256))], terms, moved=5 << 18, smem=0, late=[xp[1]])
    with jax.named_scope("dkv_over_x"):
        own = [dkv] + [send(dkv, dx=s) for s in range(1, NX)]
        other = [send(piece, dc=1) for piece in own]
    with jax.named_scope("turn_x"):
        xt, xt_give = call(turn_x_kernel, [sds((1024, 512))] * 2, (at, *xp), moved=1 << 22, late=own[1:])
        xt_other = send(xt_give, dc=1)
    with jax.named_scope("project"):
        parts = []
        for pick in (slice(0, 2), slice(2, 4)):
            n = pick.stop - pick.start
            partial = call(
                functools.partial(project_kernel, n),
                [sds((NZ, 32, 256 * n))] * 4,
                (at, xt, xt_other, *own[pick], *other[pick]),
                scratch=[pltpu.VMEM((1024, 256), F32)],
                flops=n * 5 * 10**8,
                moved=1 << 22,
                late=parts[:1],
            )
            with jax.named_scope("partial_over_y"):
                parts += [partial[0]] + [send(partial[s], dy=s) for s in range(1, NY)]
    with jax.named_scope("partial_over_z"):
        dq = [dq[0]] + [send(d, dx=-s - 1) for s, d in enumerate(after(dq[1:], [parts[1]]))]
        (summed,) = call(add_kernel, [sds((NZ, 32, 1024))], parts, moved=5 << 20, smem=0, late=dq[1:])
        groups = [[z * NC + c for z in range(NZ)] for c in range(NC)]
        last = lax.all_to_all(summed, "dp", 0, 0, axis_index_groups=groups, tiled=True)
    with jax.named_scope("grad_q"):
        (grad_q,) = call(join_q_kernel, [sds((BLK, HQ * HD))], (at, *dq), moved=1 << 21)
    with jax.named_scope("finish"):
        wk, wv = call(finish_kernel, [sds((32, 512), F32)] * 2, (at, last), moved=1 << 20)
    return grad_q, wk, wv


def solution(mesh):
    spec = P(("dp", "head"), None)
    return jax.shard_map(
        on_device,
        mesh=mesh,
        in_specs=(spec, spec, spec, spec, spec, P("dp", None)),
        out_specs=(spec, spec, spec),
        check_vma=False,
    )
```

```python
import functools
import math

import jax
import jax.numpy as jnp
from jax import lax
from jax.experimental import pallas as pl
from jax.experimental.pallas import tpu as pltpu
from jax.sharding import PartitionSpec as P

HQ = 32
HK = 4
HD = 128
BLK = 128
KB = 256
NX = 4
NY = 4
NZ = 8
NC = 2
MAX_KB = 5
SCALE = HD ** (-0.5)
LOG2E = math.log2(math.e)
BF = jnp.bfloat16
F32 = jnp.float32
AXES = ("dp", "head")
VM = pl.BlockSpec(memory_space=pltpu.VMEM)
SM = pl.BlockSpec(memory_space=pltpu.SMEM)


def send(value, dx=0, dy=0, dc=0):
    pairs = []
    for z in range(NZ):
        for c in range(NC):
            for x in range(NX):
                for y in range(NY):
                    src = ((z * NC + c) * NX + x) * NY + y
                    dst = ((z * NC + (c + dc) % NC) * NX + (x + dx) % NX) * NY + (y + dy) % NY
                    pairs.append((src, dst))
    return lax.ppermute(value, AXES, pairs)


def call(kernel, outs, ins, scratch=(), flops=0, moved=0, limit=16, smem=1, late=()):
    body = kernel
    if late:
        n, skip = len(ins), len(late)
        body = lambda *refs: kernel(*refs[:n], *refs[n + skip :])
    return pl.pallas_call(
        body,
        out_shape=outs,
        in_specs=[SM] * smem + [VM] * (len(ins) - smem) + [VM] * len(late),
        out_specs=[VM] * len(outs),
        scratch_shapes=list(scratch),
        compiler_params=pltpu.CompilerParams(vmem_limit_bytes=limit * 1024 * 1024),
        cost_estimate=pl.CostEstimate(flops=flops, bytes_accessed=moved, transcendentals=0),
    )(*ins, *late)


def sds(shape, dtype=BF):
    return jax.ShapeDtypeStruct(shape, dtype)


def pack_kv_kernel(at, k, v, *outs):
    for s in range(NX):
        first = pl.multiple_of(lax.rem(at[0] + s, NX) * HD, HD)
        outs[s][:, 0:HD] = k[:, pl.ds(first, HD)]
        outs[s][:, HD : 2 * HD] = v[:, pl.ds(first, HD)]


def join_kv_kernel(at, *refs):
    for s in range(NX):
        refs[-1][s * BLK : (s + 1) * BLK, :] = refs[s][...]


def pack_heads_kernel(at, q, do, *outs):
    group = HQ // HK
    for s in range(NX):
        first = lax.rem(at[0] + s, NX) * (group * HD)
        for h in range(group):
            col = pl.multiple_of(first + h * HD, HD)
            outs[s][0, h * BLK : (h + 1) * BLK, :] = q[:, pl.ds(col, HD)]
            outs[s][1, h * BLK : (h + 1) * BLK, :] = do[:, pl.ds(col, HD)]


def pack_x_kernel(at, li, *outs):
    for s in range(NX):
        for d in range(NC):
            core = lax.rem(at[2] + d, NC)
            for z in range(NZ):
                col = z * (NC * 512) + core * 512 + lax.rem(at[0] + s, NX) * BLK
                outs[s][d, :, z * BLK : (z + 1) * BLK] = li[:, pl.ds(pl.multiple_of(col, BLK), BLK)]


def turn_x_kernel(at, *refs):
    outs = refs[NX:]
    for d in range(NC):
        for s in range(NX):
            spot = pl.multiple_of(lax.rem(at[0] - s + NX, NX) * BLK, BLK)
            for z in range(NZ):
                rows = pl.ds(z * BLK, BLK)
                outs[d][rows, pl.ds(spot, BLK)] = refs[s][d, :, z * BLK : (z + 1) * BLK].T


def attention_kernel(pieces, at, lens, *refs):
    x, y = at[0], at[1]
    group = HQ // HK
    rows_n = group * BLK
    chunks = [slice(i * KB, (i + 1) * KB) for i in range(rows_n // KB)]
    nt = (((1,), (1,)), ((), ()))
    n = len(pieces)
    qd_in, refs = refs[0:n], refs[n:]
    if n == 3:
        kv_in, dq_out = refs[0:4], refs[4:7]
        dk, dv, k_all, v_all, kt_all, qd, s_all, dp_all, pb, dsb, dqt, dq_all = refs[7:]
        for s in range(NY):
            for t in range(NX):
                blk = NY * lax.rem(x - t + NX, NX) + lax.rem(y - s + NY, NY)
                rows = pl.ds(pl.multiple_of(blk * BLK, BLK), BLK)
                k_piece = kv_in[s][t * BLK : (t + 1) * BLK, 0:HD]
                k_all[rows, :] = k_piece
                v_all[rows, :] = kv_in[s][t * BLK : (t + 1) * BLK, HD : 2 * HD]
                kt_all[lax.div(blk, 2), :, pl.ds(pl.multiple_of(lax.rem(blk, 2) * BLK, BLK), BLK)] = k_piece.T
        dk[...] = jnp.zeros_like(dk)
        dv[...] = jnp.zeros_like(dv)
    else:
        dk_in, dv_in, k_all, v_all, kt_all = refs[0:5]
        dq_out, r_out = refs[5:6], refs[6:10]
        qd, s_all, dp_all, pb, dsb, dqt, dq_all, dk, dv = refs[10:]
        dk[...] = dk_in[...]
        dv[...] = dv_in[...]
    for i in range(n):
        qd[i] = qd_in[i][...]

    def fold(value, op):
        return op(value.reshape(KB // 8, 8, KB), axis=0)

    def query_block(j, carry):
        shift = j + lax.div(j, 2) if n == 3 else pieces[0]
        base = (NY * lax.rem(x - shift + NX, NX) + y) * BLK
        q_pos = base + (lax.broadcasted_iota(jnp.int32, (1, KB), 1) & (BLK - 1))
        start = jnp.zeros((1, KB), jnp.int32)
        first, run = jnp.int32(0), jnp.int32(0)
        for doc in range(8):
            run = run + lens[doc]
            start = jnp.maximum(start, jnp.where(q_pos >= run, run, 0))
            first = jnp.maximum(first, jnp.where(base >= run, run, 0))
        lo, hi = lax.div(first, KB), lax.div(base, KB) + 1

        def scores(kb, tops):
            keys = k_all[pl.ds(pl.multiple_of(kb * KB, KB), KB), :]
            k_pos = kb * KB + lax.broadcasted_iota(jnp.int32, (KB, KB), 0)
            keep = (k_pos >= start) & (k_pos <= q_pos)
            out = []
            for i, part in enumerate(chunks):
                s = lax.dot_general(keys, qd[j, 0, part, :], nt, preferred_element_type=F32)
                s = jnp.where(keep, s, -jnp.inf)
                s_all[kb - lo, :, part] = s
                out.append(jnp.maximum(tops[i], fold(s, jnp.max)))
            return tuple(out)

        tops = lax.fori_loop(lo, hi, scores, tuple(jnp.full((8, KB), -jnp.inf, F32) for _ in chunks))
        factor = SCALE * LOG2E
        tops = [jnp.max(t, axis=0, keepdims=True) * factor for t in tops]

        def weights(kb, sums):
            vals = v_all[pl.ds(pl.multiple_of(kb * KB, KB), KB), :]
            total, dots = [], []
            for i, part in enumerate(chunks):
                dp = lax.dot_general(vals, qd[j, 1, part, :], nt, preferred_element_type=F32)
                p = jnp.exp2(s_all[kb - lo, :, part] * factor - tops[i])
                s_all[kb - lo, :, part] = p
                dp_all[kb - lo, :, part] = dp
                total.append(sums[0][i] + fold(p, jnp.sum))
                dots.append(sums[1][i] + fold(p * dp, jnp.sum))
            return tuple(total), tuple(dots)

        zero = tuple(jnp.zeros((8, KB), F32) for _ in chunks)
        total, dots = lax.fori_loop(lo, hi, weights, (zero, zero))
        inv = [1.0 / jnp.sum(t, axis=0, keepdims=True) for t in total]
        row_dot = [jnp.sum(d, axis=0, keepdims=True) * i for d, i in zip(dots, inv)]
        dqt[...] = jnp.zeros_like(dqt)

        def grads(kb, carry):
            rows = pl.ds(pl.multiple_of(kb * KB, KB), KB)
            for i, part in enumerate(chunks):
                p = s_all[kb - lo, :, part] * inv[i]
                pb[:, part] = p.astype(BF)
                dsb[:, part] = (p * (dp_all[kb - lo, :, part] - row_dot[i])).astype(BF)
            dv[rows, :] += jnp.dot(pb[...], qd[j, 1], preferred_element_type=F32)
            dk[rows, :] += jnp.dot(dsb[...], qd[j, 0], preferred_element_type=F32)
            dqt[...] += jnp.dot(kt_all[kb], dsb[...], preferred_element_type=F32)
            return carry

        lax.fori_loop(lo, hi, grads, 0)
        for h in range(group):
            head = slice(h * BLK, (h + 1) * BLK)
            dq_all[j, head, :] = (dqt[:, head].T * SCALE).astype(BF)
        return carry

    lax.fori_loop(0, n, query_block, 0)
    for i in range(n):
        dq_out[i][...] = dq_all[i]
    if n == 3:
        return
    for s in range(NY):
        for t in range(NX):
            blk = NY * t + lax.rem(y + s, NY)
            rows = pl.ds(pl.multiple_of(blk * BLK, BLK), BLK)
            r_out[s][t * BLK : (t + 1) * BLK, 0:HD] = (dk[rows, :] * SCALE).astype(BF)
            r_out[s][t * BLK : (t + 1) * BLK, HD : 2 * HD] = dv[rows, :].astype(BF)


def join_q_kernel(at, *refs):
    out = refs[-1]
    group = HQ // HK
    for s in range(NX):
        first = lax.rem(at[0] + s, NX) * (group * HD)
        for h in range(group):
            out[:, pl.ds(pl.multiple_of(first + h * HD, HD), HD)] = refs[s][h * BLK : (h + 1) * BLK, :]


def project_kernel(pairs_n, at, xt, xt_other, *refs):
    own, other = refs[0:pairs_n], refs[pairs_n : 2 * pairs_n]
    outs, acc = refs[2 * pairs_n : 2 * pairs_n + NY], refs[-1]
    for t in range(pairs_n):
        acc[...] = jnp.dot(xt[...], own[t][...], preferred_element_type=F32) + jnp.dot(
            xt_other[...], other[t][...], preferred_element_type=F32
        )
        for s in range(NY):
            for z in range(NZ):
                row = pl.multiple_of(z * BLK + lax.rem(at[1] + s, NY) * 32, 32)
                outs[s][z, :, t * 256 : (t + 1) * 256] = acc[pl.ds(row, 32), :].astype(BF)


def add_kernel(*refs):
    out, first = refs[-1], 0
    for terms in [refs[i : i + NY] for i in range(0, len(refs) - 1, NY)]:
        wide = terms[0].shape[2]
        for z in range(NZ):
            acc = terms[0][z].astype(F32)
            for term in terms[1:]:
                acc = acc + term[z].astype(F32)
            out[z, :, first : first + wide] = acc.astype(BF)
        first += wide


def finish_kernel(at, part, wk, wv):
    for t in range(NX):
        col = pl.multiple_of(lax.rem(at[0] - t + NX, NX) * HD, HD)
        first = t * 256
        wk[:, pl.ds(col, HD)] = jnp.sum(part[:, :, first : first + HD].astype(F32), axis=0)
        wv[:, pl.ds(col, HD)] = jnp.sum(part[:, :, first + HD : first + 2 * HD].astype(F32), axis=0)


def pass_kernel(n, *refs):
    for i in range(n):
        refs[i - n][...] = refs[i][...]


def after(values, first):
    n = len(values)
    outs = [sds(v.shape, v.dtype) for v in values]
    return call(functools.partial(pass_kernel, n), outs, (*values, *first), moved=1024, smem=0)


def split(n, values):
    return list(values[:n]), list(values[n:])


def sum_kernel(*refs):
    acc = refs[0][...].astype(F32)
    for ref in refs[1:NY]:
        acc = acc + ref[...].astype(F32)
    refs[-1][...] = acc.astype(BF)


def on_device(layer_input, queries, key_rows, value_rows, d_out, doc_lengths):
    head, dp = lax.axis_index("head"), lax.axis_index("dp")
    at = jnp.stack([head // NY, head % NY, dp % NC, dp // NC]).astype(jnp.int32)
    with jax.named_scope("pack_kv"):
        kv = call(pack_kv_kernel, [sds((BLK, 256))] * 4, (at, key_rows, value_rows), moved=1 << 19)
    with jax.named_scope("pack_q_do"):
        qd = call(pack_heads_kernel, [sds((2, 1024, HD))] * 4, (at, queries, d_out), moved=1 << 22, late=[kv[1]])
    with jax.named_scope("kv_over_x"):
        kv = [kv[0]] + [send(kv[s], dx=s) for s in range(1, NX)]
        qd = [qd[0], *after(qd[1:], kv[1:])]
        (kv,) = call(join_kv_kernel, [sds((512, 256))], (at, *kv), moved=1 << 19, late=[qd[1]])
    with jax.named_scope("pack_x"):
        xp = call(pack_x_kernel, [sds((NC, BLK, 1024))] * 4, (at, layer_input), moved=1 << 22, late=[kv])
    with jax.named_scope("q_do_over_x"):
        qd = [qd[0]] + [send(qd[s], dx=s) for s in range(1, NX)]
    with jax.named_scope("kv_over_y"):
        kv = [kv] + [send(kv, dy=s) for s in range(1, NY)]
    with jax.named_scope("attention"):
        held = [sds((2048, HD), F32)] * 2 + [sds((2048, HD))] * 2 + [sds((8, HD, KB))]
        def scratch(n):
            return [
                pltpu.VMEM((n, 2, 1024, HD), BF),
                pltpu.VMEM((MAX_KB, KB, 1024), F32),
                pltpu.VMEM((MAX_KB, KB, 1024), F32),
                pltpu.VMEM((KB, 1024), BF),
                pltpu.VMEM((KB, 1024), BF),
                pltpu.VMEM((HD, 1024), F32),
                pltpu.VMEM((n, 1024, HD), BF),
            ]

        (dq0, dq1, dq3), held = split(
            3,
            call(
                functools.partial(attention_kernel, (0, 1, 3)),
                [sds((1024, HD))] * 3 + held,
                (at, doc_lengths[0], qd[0], qd[1], qd[3], *kv),
                scratch=scratch(3),
                flops=12 * 10**9,
                moved=6 << 20,
                limit=32,
                smem=2,
            ),
        )
        (dq2,), terms = split(
            1,
            call(
                functools.partial(attention_kernel, (2,)),
                [sds((1024, HD))] + [sds((512, 256))] * 4,
                (at, doc_lengths[0], qd[2], *held),
                scratch=scratch(1) + [pltpu.VMEM((2048, HD), F32)] * 2,
                flops=4 * 10**9,
                moved=6 << 20,
                limit=32,
                smem=2,
            ),
        )
    dq = [dq0, dq1, dq2, dq3]
    with jax.named_scope("terms_over_y"):
        give = after(xp[1:], terms[:1])
        terms = [terms[0]] + [send(terms[s], dy=s) for s in range(1, NY)]
        xp = [xp[0]] + [send(d, dx=s + 1) for s, d in enumerate(give)]
        (dkv,) = call(sum_kernel, [sds((512, 256))], terms, moved=5 << 18, smem=0, late=[xp[1]])
    with jax.named_scope("dkv_over_x"):
        own = [dkv] + [send(dkv, dx=s) for s in range(1, NX)]
        other = [send(piece, dc=1) for piece in own[:2]]
    with jax.named_scope("turn_x"):
        xt, xt_give = call(turn_x_kernel, [sds((1024, 512))] * 2, (at, *xp), moved=1 << 22, late=own[1:2])
        xt_other = send(xt_give, dc=1)
    with jax.named_scope("project"):
        parts = []
        for pick in (slice(0, 2), slice(2, 4)):
            n = pick.stop - pick.start
            partial = call(
                functools.partial(project_kernel, n),
                [sds((NZ, 32, 256 * n))] * 4,
                (at, xt, xt_other, *own[pick], *other[pick]),
                scratch=[pltpu.VMEM((1024, 256), F32)],
                flops=n * 5 * 10**8,
                moved=1 << 22,
                late=parts[:1],
            )
            with jax.named_scope("partial_over_y"):
                parts += [partial[0]] + [send(partial[s], dy=s) for s in range(1, NY)]
            if len(other) == 2:
                other += [send(piece, dc=1) for piece in after(own[2:], parts[1:])]
    with jax.named_scope("partial_over_z"):
        dq = [dq[0]] + [send(d, dx=-s - 1) for s, d in enumerate(after(dq[1:], [parts[5]]))]
        (summed,) = call(add_kernel, [sds((NZ, 32, 1024))], parts, moved=5 << 20, smem=0, late=dq[1:])
        groups = [[z * NC + c for z in range(NZ)] for c in range(NC)]
        last = lax.all_to_all(summed, "dp", 0, 0, axis_index_groups=groups, tiled=True)
    with jax.named_scope("grad_q"):
        (grad_q,) = call(join_q_kernel, [sds((BLK, HQ * HD))], (at, *dq), moved=1 << 21)
    with jax.named_scope("finish"):
        wk, wv = call(finish_kernel, [sds((32, 512), F32)] * 2, (at, last), moved=1 << 20)
    return grad_q, wk, wv


def solution(mesh):
    spec = P(("dp", "head"), None)
    return jax.shard_map(
        on_device,
        mesh=mesh,
        in_specs=(spec, spec, spec, spec, spec, P("dp", None)),
        out_specs=(spec, spec, spec),
        check_vma=False,
    )
```

```python
import functools
import math

import jax
import jax.numpy as jnp
from jax import lax
from jax.experimental import pallas as pl
from jax.experimental.pallas import tpu as pltpu
from jax.sharding import PartitionSpec as P

HQ = 32
HK = 4
HD = 128
BLK = 128
KB = 256
NX = 4
NY = 4
NZ = 8
NC = 2
MAX_KB = 5
SCALE = HD ** (-0.5)
LOG2E = math.log2(math.e)
BF = jnp.bfloat16
F32 = jnp.float32
AXES = ("dp", "head")
VM = pl.BlockSpec(memory_space=pltpu.VMEM)
SM = pl.BlockSpec(memory_space=pltpu.SMEM)


def send(value, dx=0, dy=0, dc=0):
    pairs = []
    for z in range(NZ):
        for c in range(NC):
            for x in range(NX):
                for y in range(NY):
                    src = ((z * NC + c) * NX + x) * NY + y
                    dst = ((z * NC + (c + dc) % NC) * NX + (x + dx) % NX) * NY + (y + dy) % NY
                    pairs.append((src, dst))
    return lax.ppermute(value, AXES, pairs)


def call(kernel, outs, ins, scratch=(), flops=0, moved=0, limit=16, smem=1, late=()):
    body = kernel
    if late:
        n, skip = len(ins), len(late)
        body = lambda *refs: kernel(*refs[:n], *refs[n + skip :])
    return pl.pallas_call(
        body,
        out_shape=outs,
        in_specs=[SM] * smem + [VM] * (len(ins) - smem) + [VM] * len(late),
        out_specs=[VM] * len(outs),
        scratch_shapes=list(scratch),
        compiler_params=pltpu.CompilerParams(vmem_limit_bytes=limit * 1024 * 1024),
        cost_estimate=pl.CostEstimate(flops=flops, bytes_accessed=moved, transcendentals=0),
    )(*ins, *late)


def sds(shape, dtype=BF):
    return jax.ShapeDtypeStruct(shape, dtype)


def pack_kv_kernel(at, k, v, *outs):
    for s in range(NX):
        first = pl.multiple_of(lax.rem(at[0] + s, NX) * HD, HD)
        outs[s][:, 0:HD] = k[:, pl.ds(first, HD)]
        outs[s][:, HD : 2 * HD] = v[:, pl.ds(first, HD)]


def join_kv_kernel(at, *refs):
    for s in range(NX):
        refs[-1][s * BLK : (s + 1) * BLK, :] = refs[s][...]


def pack_heads_kernel(at, q, do, *outs):
    group = HQ // HK
    for s in range(NX):
        first = lax.rem(at[0] + s, NX) * (group * HD)
        for h in range(group):
            col = pl.multiple_of(first + h * HD, HD)
            outs[s][0, h * BLK : (h + 1) * BLK, :] = q[:, pl.ds(col, HD)]
            outs[s][1, h * BLK : (h + 1) * BLK, :] = do[:, pl.ds(col, HD)]


def pack_x_kernel(at, li, *outs):
    for s in range(NX):
        for d in range(NC):
            core = lax.rem(at[2] + d, NC)
            for z in range(NZ):
                col = z * (NC * 512) + core * 512 + lax.rem(at[0] + s, NX) * BLK
                outs[s][d, :, z * BLK : (z + 1) * BLK] = li[:, pl.ds(pl.multiple_of(col, BLK), BLK)]


def turn_x_kernel(at, *refs):
    outs = refs[NX:]
    for d in range(NC):
        for s in range(NX):
            spot = pl.multiple_of(lax.rem(at[0] - s + NX, NX) * BLK, BLK)
            for z in range(NZ):
                rows = pl.ds(z * BLK, BLK)
                outs[d][rows, pl.ds(spot, BLK)] = refs[s][d, :, z * BLK : (z + 1) * BLK].T


def attention_kernel(first_piece, at, lens, *refs):
    x, y = at[0], at[1]
    group = HQ // HK
    rows_n = group * BLK
    chunks = [slice(i * KB, (i + 1) * KB) for i in range(rows_n // KB)]
    nt = (((1,), (1,)), ((), ()))
    qd_in, refs = refs[0:2], refs[2:]
    if first_piece == 0:
        kv_in, dq_out = refs[0:4], refs[4:6]
        dk, dv, k_all, v_all, kt_all, qd, s_all, dp_all, pb, dsb, dqt, dq_all = refs[6:]
        for s in range(NY):
            for t in range(NX):
                blk = NY * lax.rem(x - t + NX, NX) + lax.rem(y - s + NY, NY)
                rows = pl.ds(pl.multiple_of(blk * BLK, BLK), BLK)
                k_piece = kv_in[s][t * BLK : (t + 1) * BLK, 0:HD]
                k_all[rows, :] = k_piece
                v_all[rows, :] = kv_in[s][t * BLK : (t + 1) * BLK, HD : 2 * HD]
                kt_all[lax.div(blk, 2), :, pl.ds(pl.multiple_of(lax.rem(blk, 2) * BLK, BLK), BLK)] = k_piece.T
        dk[...] = jnp.zeros_like(dk)
        dv[...] = jnp.zeros_like(dv)
    else:
        dk_in, dv_in, k_all, v_all, kt_all = refs[0:5]
        dq_out, r_out = refs[5:7], refs[7:11]
        qd, s_all, dp_all, pb, dsb, dqt, dq_all, dk, dv = refs[11:]
        dk[...] = dk_in[...]
        dv[...] = dv_in[...]
    for s in range(2):
        qd[s] = qd_in[s][...]

    def fold(value, op):
        return op(value.reshape(KB // 8, 8, KB), axis=0)

    def query_block(j, carry):
        base = (NY * lax.rem(x - j - first_piece + NX, NX) + y) * BLK
        q_pos = base + (lax.broadcasted_iota(jnp.int32, (1, KB), 1) & (BLK - 1))
        start = jnp.zeros((1, KB), jnp.int32)
        first, run = jnp.int32(0), jnp.int32(0)
        for n in range(8):
            run = run + lens[n]
            start = jnp.maximum(start, jnp.where(q_pos >= run, run, 0))
            first = jnp.maximum(first, jnp.where(base >= run, run, 0))
        lo, hi = lax.div(first, KB), lax.div(base, KB) + 1

        def scores(kb, tops):
            keys = k_all[pl.ds(pl.multiple_of(kb * KB, KB), KB), :]
            k_pos = kb * KB + lax.broadcasted_iota(jnp.int32, (KB, KB), 0)
            keep = (k_pos >= start) & (k_pos <= q_pos)
            out = []
            for i, part in enumerate(chunks):
                s = lax.dot_general(keys, qd[j, 0, part, :], nt, preferred_element_type=F32)
                s = jnp.where(keep, s, -jnp.inf)
                s_all[kb - lo, :, part] = s
                out.append(jnp.maximum(tops[i], fold(s, jnp.max)))
            return tuple(out)

        tops = lax.fori_loop(lo, hi, scores, tuple(jnp.full((8, KB), -jnp.inf, F32) for _ in chunks))
        factor = SCALE * LOG2E
        tops = [jnp.max(t, axis=0, keepdims=True) * factor for t in tops]

        def weights(kb, sums):
            vals = v_all[pl.ds(pl.multiple_of(kb * KB, KB), KB), :]
            total, dots = [], []
            for i, part in enumerate(chunks):
                dp = lax.dot_general(vals, qd[j, 1, part, :], nt, preferred_element_type=F32)
                p = jnp.exp2(s_all[kb - lo, :, part] * factor - tops[i])
                s_all[kb - lo, :, part] = p
                dp_all[kb - lo, :, part] = dp
                total.append(sums[0][i] + fold(p, jnp.sum))
                dots.append(sums[1][i] + fold(p * dp, jnp.sum))
            return tuple(total), tuple(dots)

        zero = tuple(jnp.zeros((8, KB), F32) for _ in chunks)
        total, dots = lax.fori_loop(lo, hi, weights, (zero, zero))
        inv = [1.0 / jnp.sum(t, axis=0, keepdims=True) for t in total]
        row_dot = [jnp.sum(d, axis=0, keepdims=True) * i for d, i in zip(dots, inv)]
        dqt[...] = jnp.zeros_like(dqt)

        def grads(kb, carry):
            rows = pl.ds(pl.multiple_of(kb * KB, KB), KB)
            for i, part in enumerate(chunks):
                p = s_all[kb - lo, :, part] * inv[i]
                pb[:, part] = p.astype(BF)
                dsb[:, part] = (p * (dp_all[kb - lo, :, part] - row_dot[i])).astype(BF)
            dv[rows, :] += jnp.dot(pb[...], qd[j, 1], preferred_element_type=F32)
            dk[rows, :] += jnp.dot(dsb[...], qd[j, 0], preferred_element_type=F32)
            dqt[...] += jnp.dot(kt_all[kb], dsb[...], preferred_element_type=F32)
            return carry

        lax.fori_loop(lo, hi, grads, 0)
        for h in range(group):
            head = slice(h * BLK, (h + 1) * BLK)
            dq_all[j, head, :] = (dqt[:, head].T * SCALE).astype(BF)
        return carry

    lax.fori_loop(0, 2, query_block, 0)
    for s in range(2):
        dq_out[s][...] = dq_all[s]
    if first_piece == 0:
        return
    for s in range(NY):
        for t in range(NX):
            blk = NY * t + lax.rem(y + s, NY)
            rows = pl.ds(pl.multiple_of(blk * BLK, BLK), BLK)
            r_out[s][t * BLK : (t + 1) * BLK, 0:HD] = (dk[rows, :] * SCALE).astype(BF)
            r_out[s][t * BLK : (t + 1) * BLK, HD : 2 * HD] = dv[rows, :].astype(BF)


def join_q_kernel(at, *refs):
    out = refs[-1]
    group = HQ // HK
    for s in range(NX):
        first = lax.rem(at[0] + s, NX) * (group * HD)
        for h in range(group):
            out[:, pl.ds(pl.multiple_of(first + h * HD, HD), HD)] = refs[s][h * BLK : (h + 1) * BLK, :]


def project_kernel(pairs_n, at, xt, xt_other, *refs):
    own, other = refs[0:pairs_n], refs[pairs_n : 2 * pairs_n]
    outs, acc = refs[2 * pairs_n : 2 * pairs_n + NY], refs[-1]
    for t in range(pairs_n):
        acc[...] = jnp.dot(xt[...], own[t][...], preferred_element_type=F32) + jnp.dot(
            xt_other[...], other[t][...], preferred_element_type=F32
        )
        for s in range(NY):
            for z in range(NZ):
                row = pl.multiple_of(z * BLK + lax.rem(at[1] + s, NY) * 32, 32)
                outs[s][z, :, t * 256 : (t + 1) * 256] = acc[pl.ds(row, 32), :].astype(BF)


def add_kernel(*refs):
    out, first = refs[-1], 0
    for terms in [refs[i : i + NY] for i in range(0, len(refs) - 1, NY)]:
        wide = terms[0].shape[2]
        for z in range(NZ):
            acc = terms[0][z].astype(F32)
            for term in terms[1:]:
                acc = acc + term[z].astype(F32)
            out[z, :, first : first + wide] = acc.astype(BF)
        first += wide


def finish_kernel(at, part, wk, wv):
    for t in range(NX):
        col = pl.multiple_of(lax.rem(at[0] - t + NX, NX) * HD, HD)
        first = t * 256
        wk[:, pl.ds(col, HD)] = jnp.sum(part[:, :, first : first + HD].astype(F32), axis=0)
        wv[:, pl.ds(col, HD)] = jnp.sum(part[:, :, first + HD : first + 2 * HD].astype(F32), axis=0)


def pass_kernel(n, *refs):
    for i in range(n):
        refs[i - n][...] = refs[i][...]


def after(values, first):
    n = len(values)
    outs = [sds(v.shape, v.dtype) for v in values]
    return call(functools.partial(pass_kernel, n), outs, (*values, *first), moved=1024, smem=0)


def split(n, values):
    return list(values[:n]), list(values[n:])


def total(values):
    acc = values[0].astype(F32)
    for value in values[1:]:
        acc = acc + value.astype(F32)
    return acc.astype(BF)


def on_device(layer_input, queries, key_rows, value_rows, d_out, doc_lengths):
    head, dp = lax.axis_index("head"), lax.axis_index("dp")
    at = jnp.stack([head // NY, head % NY, dp % NC, dp // NC]).astype(jnp.int32)
    with jax.named_scope("pack_kv"):
        kv = call(pack_kv_kernel, [sds((BLK, 256))] * 4, (at, key_rows, value_rows), moved=1 << 19)
    with jax.named_scope("pack_q_do"):
        qd = call(pack_heads_kernel, [sds((2, 1024, HD))] * 4, (at, queries, d_out), moved=1 << 22, late=[kv[1]])
    with jax.named_scope("kv_over_x"):
        kv = [kv[0]] + [send(kv[s], dx=s) for s in range(1, NX)]
        qd = [qd[0], *after(qd[1:], kv[1:])]
        (kv,) = call(join_kv_kernel, [sds((512, 256))], (at, *kv), moved=1 << 19, late=[qd[1]])
    with jax.named_scope("pack_x"):
        xp = call(pack_x_kernel, [sds((NC, BLK, 1024))] * 4, (at, layer_input), moved=1 << 22, late=[kv])
    with jax.named_scope("q_do_over_x"):
        qd = [qd[0]] + [send(qd[s], dx=s) for s in range(1, NX)]
    with jax.named_scope("kv_over_y"):
        kv = [kv] + [send(kv, dy=s) for s in range(1, NY)]
    with jax.named_scope("attention"):
        held = [sds((2048, HD), F32)] * 2 + [sds((2048, HD))] * 2 + [sds((8, HD, KB))]
        scratch = [
            pltpu.VMEM((2, 2, 1024, HD), BF),
            pltpu.VMEM((MAX_KB, KB, 1024), F32),
            pltpu.VMEM((MAX_KB, KB, 1024), F32),
            pltpu.VMEM((KB, 1024), BF),
            pltpu.VMEM((KB, 1024), BF),
            pltpu.VMEM((HD, 1024), F32),
            pltpu.VMEM((2, 1024, HD), BF),
        ]
        dq_a, held = split(
            2,
            call(
                functools.partial(attention_kernel, 0),
                [sds((1024, HD))] * 2 + held,
                (at, doc_lengths[0], *qd[:2], *kv),
                scratch=scratch,
                flops=8 * 10**9,
                moved=6 << 20,
                limit=32,
                smem=2,
            ),
        )
        give = after(xp[1:], [dq_a[0], qd[2]])
        xp = [xp[0]] + [send(d, dx=s + 1) for s, d in enumerate(give)]
        dq_b, terms = split(
            2,
            call(
                functools.partial(attention_kernel, 2),
                [sds((1024, HD))] * 2 + [sds((512, 256))] * 4,
                (at, doc_lengths[0], *qd[2:], *held),
                scratch=scratch + [pltpu.VMEM((2048, HD), F32)] * 2,
                flops=8 * 10**9,
                moved=6 << 20,
                limit=32,
                smem=2,
                late=give[:1],
            ),
        )
    dq = dq_a + dq_b
    with jax.named_scope("terms_over_y"):
        terms = [terms[0]] + [send(d, dy=s + 1) for s, d in enumerate(after(terms[1:], [xp[1]]))]
        dkv = total(terms)
    with jax.named_scope("turn_x"):
        xt, xt_give = call(turn_x_kernel, [sds((1024, 512))] * 2, (at, *xp), moved=1 << 22, late=terms[1:])
        xt_other = send(xt_give, dc=1)
    with jax.named_scope("dkv_over_x"):
        own = [dkv] + [send(dkv, dx=s) for s in range(1, NX)]
        other = [send(piece, dc=1) for piece in own[:2]]
    with jax.named_scope("project"):
        parts = []
        for pick in (slice(0, 1), slice(1, 4)):
            n = pick.stop - pick.start
            partial = call(
                functools.partial(project_kernel, n),
                [sds((NZ, 32, 256 * n))] * 4,
                (at, xt, xt_other, *own[pick], *other[pick]),
                scratch=[pltpu.VMEM((1024, 256), F32)],
                flops=n * 5 * 10**8,
                moved=1 << 22,

            )
            with jax.named_scope("partial_over_y"):
                parts += [partial[0]] + [send(partial[s], dy=s) for s in range(1, NY)]
            if len(other) == 2:
                other += [send(piece, dc=1) for piece in after(own[2:], parts[1:])]
    with jax.named_scope("partial_over_z"):
        dq = [dq[0]] + [send(d, dx=-s - 1) for s, d in enumerate(after(dq[1:], [parts[4]]))]
        (summed,) = call(add_kernel, [sds((NZ, 32, 1024))], parts, moved=5 << 20, smem=0, late=dq[1:2])
        groups = [[z * NC + c for z in range(NZ)] for c in range(NC)]
        last = lax.all_to_all(summed, "dp", 0, 0, axis_index_groups=groups, tiled=True)
    with jax.named_scope("grad_q"):
        (grad_q,) = call(join_q_kernel, [sds((BLK, HQ * HD))], (at, *dq), moved=1 << 21)
    with jax.named_scope("finish"):
        wk, wv = call(finish_kernel, [sds((32, 512), F32)] * 2, (at, last), moved=1 << 20)
    return grad_q, wk, wv


def solution(mesh):
    spec = P(("dp", "head"), None)
    return jax.shard_map(
        on_device,
        mesh=mesh,
        in_specs=(spec, spec, spec, spec, spec, P("dp", None)),
        out_specs=(spec, spec, spec),
        check_vma=False,
    )
```
